32 devices in a mesh: sub: 2 (over x), dev: 16 (over z, y, core).
Axes of the slice: x: 2, y: 2, z: 4, core: 2. Of those that a mesh axis runs over, the one named last changes fastest.
Arguments:
- root_rhs: bfloat16 [256, 16384], P('dev', 'sub'), may hold values from -6 to 6
- root_inverse: bfloat16 [128, 128, 128], P('sub')
- level_rhs: bfloat16 [256, 4096], P(None, ('sub', 'dev')), may hold values from -6 to 6
- level_inverse: bfloat16 [32, 128, 128], P(('sub', 'dev'))
- level_panels: bfloat16 [32, 16, 128, 128], P(('sub', 'dev')), may hold values from -0.125 to 0.125
- level_columns: int32 [32, 16], P(('sub', 'dev')), may hold values from 0 to 127, as said below
- leaf_rhs: bfloat16 [256, 262144], P(None, ('sub', 'dev')), may hold values from -6 to 6
- leaf_inverse: bfloat16 [2048, 128, 128], P(('sub', 'dev'))
- leaf_panels: bfloat16 [2048, 6, 128, 128], P(('sub', 'dev')), may hold values from -0.21875 to 0.21875
- leaf_columns: int32 [2048, 6], P(('sub', 'dev')), may hold values from 0 to 143, as said below
- slab_order: int32 [32, 64], P(('sub', 'dev')), may hold values from 0 to 63, each once within a row
Outputs:
- slab_adjoint: bfloat16 [256, 262144], P(None, ('sub', 'dev'))
The draws below stay inside these ranges and needn't reach their ends.
Inputs may be any that keep to these rules, and one draw needn't show every extreme that they name: `level_columns`: entries of one row are distinct. `leaf_columns`: entries of one row are distinct; values under 128 name top-separator blocks, the others second-level blocks of the device's own subcube. `slab_order`: each row is a permutation.
All inputs are finite; a program needn't handle non-finite values.
Results may differ from the reference program's by a relative error of at most 0.0059.
Values may be sent and summed in bfloat16 or wider, within the bound.
No kernel may reach another device: no remote copies, remote signals or barrier semaphores. Data moves between devices by JAX's collectives and lax.ppermute only.
A program may use at most 256 MiB of HBM per device.

```python
import jax
import jax.numpy as jnp
from jax import lax

BLOCK = 128
ROOT_BLOCKS = 128
LEVEL_TILES = 16
LEAF_TILES = 6
LEAF_BLOCKS = 64
RHS = 256
ROOT_ROWS = 16384
LEVEL_BLOCKS = 16
LEVEL_ROWS = 2048
LEAF_ROWS = 8192
GROUPS = 32
N_SUB = 2
N_DEV = 16


def inverse_blocks(key, block_count):
    diag_key, off_key = jax.random.split(key)
    diagonal = jax.random.uniform(diag_key, (block_count, BLOCK), jnp.float32, 0.6, 1.4)
    off_part = jax.random.normal(off_key, (block_count, BLOCK, BLOCK), jnp.float32) * (0.6 / BLOCK ** 0.5)
    identity = jnp.eye(BLOCK, dtype=jnp.float32)
    return off_part * (1.0 - identity) + diagonal[:, :, None] * identity


def distinct_picks(key, row_count, options, picks):
    scores = jax.random.randint(key, (row_count, options), 0, 1 << 20) * options + jnp.arange(options, dtype=jnp.int32)
    return lax.top_k(scores, picks)[1].astype(jnp.int32)


def draw_root_inverse(key, part):
    return inverse_blocks(key, ROOT_BLOCKS).astype(jnp.bfloat16)


def draw_level_inverse(key, part):
    return inverse_blocks(key, GROUPS).astype(jnp.bfloat16)


def draw_leaf_inverse(key, part):
    return inverse_blocks(key, GROUPS * LEAF_BLOCKS).astype(jnp.bfloat16)


def draw_level_columns(key, part):
    return distinct_picks(key, GROUPS, ROOT_BLOCKS, LEVEL_TILES)


def draw_leaf_columns(key, part):
    return distinct_picks(key, GROUPS * LEAF_BLOCKS, ROOT_BLOCKS + LEVEL_BLOCKS, LEAF_TILES)


def steps_of(key, extent, cuts, smallest, largest):
    level = 1.0
    for dim, parts in cuts:
        heights = jax.random.uniform(jax.random.fold_in(jax.random.fold_in(key, 6), dim), (parts,), jnp.float32, smallest / len(cuts), largest / len(cuts))
        level = level * jnp.repeat(jnp.exp(heights), extent[dim] // parts).reshape((-1,) + (1,) * (len(extent) - 1 - dim))
    return level


def scatter_about(rng, dims, deviation, reach, cuts=(), kind=jnp.bfloat16):
    entries = jax.random.normal(rng, dims, jnp.float32) * deviation
    if len(cuts) > 0:
        entries = steps_of(rng, dims, cuts, -0.22, 0.18) * entries
    return jnp.clip(entries, min=-reach, max=reach).astype(kind)


def setup_inputs(seed: int = 0) -> dict:
    key_of = jax.random.split(jax.random.key(seed), 12)
    return {
        "root_rhs": scatter_about(key_of[0], (RHS, ROOT_ROWS), 1.0, 6.0, ((0, 16), (1, 2))),
        "root_inverse": draw_root_inverse(jax.random.fold_in(key_of[11], 71), 0),
        "level_rhs": scatter_about(key_of[2], (RHS, N_SUB * LEVEL_ROWS), 1.0, 6.0, ((1, 32),)),
        "level_inverse": draw_level_inverse(jax.random.fold_in(key_of[11], 71), 0),
        "level_panels": scatter_about(key_of[4], (GROUPS, LEVEL_TILES, BLOCK, BLOCK), (LEVEL_TILES * BLOCK) ** -0.5, 0.125, ((0, 32),)),
        "level_columns": draw_level_columns(jax.random.fold_in(key_of[11], 71), 0),
        "leaf_rhs": scatter_about(key_of[6], (RHS, GROUPS * LEAF_ROWS), 1.0, 6.0, ((1, 32),)),
        "leaf_inverse": draw_leaf_inverse(jax.random.fold_in(key_of[11], 71), 0),
        "leaf_panels": scatter_about(key_of[8], (GROUPS * LEAF_BLOCKS, LEAF_TILES, BLOCK, BLOCK), (LEAF_TILES * BLOCK) ** -0.5, 0.21875, ((0, 32),)),
        "leaf_columns": draw_leaf_columns(jax.random.fold_in(key_of[11], 71), 0),
        "slab_order": jax.vmap(lambda own: jax.random.permutation(own, LEAF_BLOCKS))(jax.random.split(key_of[10], GROUPS)).reshape((GROUPS, LEAF_BLOCKS)).astype(jnp.int32),
    }


def apply_inverse(inverse, vector):
    row_count = vector.shape[0]
    block_count = inverse.shape[0]
    block_width = inverse.shape[1]
    pieces = vector.reshape(row_count, block_count, block_width).astype(jnp.float32)
    result = jnp.einsum('rnj,nij->rni', pieces, inverse.astype(jnp.float32))
    return result.reshape(row_count, block_count * block_width)


def gather_blocks(panels, columns, source):
    row_count = source.shape[0]
    block_count = panels.shape[0]
    tile_depth = panels.shape[1]
    block_width = panels.shape[2]
    blocks = source.reshape(row_count, -1, block_width)
    picked = jnp.take(blocks, columns.reshape(-1).astype(jnp.int32), axis=1)
    picked = picked.reshape(row_count, block_count, tile_depth, block_width).astype(jnp.float32)
    result = jnp.einsum('rnkj,nkij->rni', picked, panels.astype(jnp.float32))
    return result.reshape(row_count, block_count * block_width)


def reference(root_rhs, root_inverse, level_rhs, level_inverse, level_panels, level_columns, leaf_rhs, leaf_inverse, leaf_panels, leaf_columns, slab_order):
    root_sol = apply_inverse(root_inverse, root_rhs).astype(jnp.bfloat16)
    level_rhs_g = level_rhs.reshape(RHS, N_SUB, N_DEV * BLOCK).transpose(1, 0, 2)
    level_inv_g = level_inverse.reshape(N_SUB, N_DEV, BLOCK, BLOCK)
    level_pan_g = level_panels.reshape(N_SUB, N_DEV, LEVEL_TILES, BLOCK, BLOCK)
    level_col_g = level_columns.reshape(N_SUB, N_DEV, LEVEL_TILES)

    def level_solve(inputs):
        rhs_part, inverse, panels, columns = inputs
        partial_sum = gather_blocks(panels, columns, root_sol)
        residue = (rhs_part.astype(jnp.float32) - partial_sum).astype(jnp.bfloat16)
        return apply_inverse(inverse, residue).astype(jnp.bfloat16)

    level_sol = lax.map(level_solve, (level_rhs_g, level_inv_g, level_pan_g, level_col_g))
    leaf_rhs_g = leaf_rhs.reshape(RHS, N_SUB, N_DEV, LEAF_ROWS).transpose(1, 2, 0, 3)
    leaf_inv_g = leaf_inverse.reshape(N_SUB, N_DEV, LEAF_BLOCKS, BLOCK, BLOCK)
    leaf_pan_g = leaf_panels.reshape(N_SUB, N_DEV, LEAF_BLOCKS, LEAF_TILES, BLOCK, BLOCK)
    leaf_col_g = leaf_columns.reshape(N_SUB, N_DEV, LEAF_BLOCKS, LEAF_TILES)

    def group_solve(inputs):
        rhs_group, inv_group, pan_group, col_group, level_group = inputs
        source = jnp.concatenate([root_sol, level_group], axis=1)

        def device_solve(device_inputs):
            rhs_part, inverse, panels, columns = device_inputs
            partial_sum = gather_blocks(panels, columns, source)
            residue = (rhs_part.astype(jnp.float32) - partial_sum).astype(jnp.bfloat16)
            return apply_inverse(inverse, residue).astype(jnp.bfloat16)

        return lax.map(device_solve, (rhs_group, inv_group, pan_group, col_group))

    leaf_sol = lax.map(group_solve, (leaf_rhs_g, leaf_inv_g, leaf_pan_g, leaf_col_g, level_sol))
    tile_set = leaf_sol.reshape(N_SUB, N_DEV, RHS, LEAF_BLOCKS, BLOCK)
    order_rows = slab_order.reshape(N_SUB, N_DEV, LEAF_BLOCKS).astype(jnp.int32)

    def pick_tiles(tiles_one, order_one):
        return jnp.take(tiles_one, order_one, axis=1)

    chosen = jax.vmap(jax.vmap(pick_tiles))(tile_set, order_rows)
    spread = LEAF_BLOCKS // N_DEV
    chosen = chosen.reshape(N_SUB, N_DEV, RHS, N_DEV, spread, BLOCK)
    return chosen.transpose(2, 0, 3, 1, 4, 5).reshape(RHS, N_SUB * N_DEV * LEAF_ROWS)
```

```python
import functools

import jax
import jax.numpy as jnp
from jax import lax
from jax.experimental import pallas as pl
from jax.experimental.pallas import tpu as pltpu
from jax.sharding import PartitionSpec as P

NT = (((1,), (1,)), ((), ()))


def load_source(copies):
    for copy in copies:
        copy.start()
    for copy in copies:
        copy.wait()


def pick_product(source, columns, panels):
    groups, _, rows, width = source.shape
    picked = [source[:, col].reshape(groups * rows, width) for col in columns]
    total = None
    step = 2 if len(picked) % 2 == 0 else 1
    for k in range(0, len(picked), step):
        left = jnp.concatenate(picked[k : k + step], axis=1)
        right = jnp.concatenate(panels[k : k + step], axis=1)
        term = lax.dot_general(left, right, NT, preferred_element_type=jnp.float32)
        total = term if total is None else total + term
    return total


def solve_block(rhs, part, inverse):
    residue = (rhs.astype(jnp.float32) - part).astype(jnp.bfloat16)
    return lax.dot_general(
        residue, inverse, NT, preferred_element_type=jnp.float32
    ).astype(jnp.bfloat16)


def level_kernel(columns, root_hbm, rhs, panels, inverse, out, source, sems):
    subs, groups, blocks = root_hbm.shape[:3]
    copies = []
    for s in range(subs):
        for e in range(groups):
            copies.append(
                pltpu.make_async_copy(
                    root_hbm.at[s, e],
                    source.at[e, pl.ds(s * blocks, blocks)],
                    sems.at[s * groups + e],
                )
            )
    load_source(copies)
    tiles = panels.shape[1]
    part = pick_product(
        source,
        [columns[0, k] for k in range(tiles)],
        [panels[0, k] for k in range(tiles)],
    )
    shape = rhs.shape
    solved = solve_block(rhs[...].reshape(part.shape), part, inverse[0])
    out[...] = solved.reshape(shape)


def level_solve(root, rhs, panels, inverse, columns):
    subs, groups, blocks, rows, width = root.shape
    vmem = pl.BlockSpec(memory_space=pltpu.VMEM)
    return pl.pallas_call(
        level_kernel,
        out_shape=jax.ShapeDtypeStruct((groups, rows, width), jnp.bfloat16),
        in_specs=[
            pl.BlockSpec(memory_space=pltpu.SMEM),
            pl.BlockSpec(memory_space=pl.ANY),
            vmem,
            vmem,
            vmem,
        ],
        out_specs=vmem,
        scratch_shapes=[
            pltpu.VMEM((groups, subs * blocks, rows, width), jnp.bfloat16),
            pltpu.SemaphoreType.DMA((subs * groups,)),
        ],
        compiler_params=pltpu.CompilerParams(vmem_limit_bytes=40 * 2**20),
        name="level_solve",
    )(columns, root, rhs.reshape(groups, rows, width), panels, inverse)


def leaf_kernel(per_step, order, columns, root_hbm, level_hbm, *refs):
    rhs = refs[:per_step]
    panels = refs[per_step : 2 * per_step]
    inverse = refs[2 * per_step : 3 * per_step]
    out, source, sems = refs[3 * per_step :]
    subs, groups, blocks = root_hbm.shape[:3]
    level_blocks = level_hbm.shape[0]
    step = pl.program_id(0)

    @pl.when(step == 0)
    def _():
        copies = []
        for s in range(subs):
            for e in range(groups):
                copies.append(
                    pltpu.make_async_copy(
                        root_hbm.at[s, e],
                        source.at[e, pl.ds(s * blocks, blocks)],
                        sems.at[s * groups + e],
                    )
                )
        for j in range(level_blocks):
            copies.append(
                pltpu.make_async_copy(
                    level_hbm.at[j],
                    source.at[:, subs * blocks + j],
                    sems.at[subs * groups + j],
                )
            )
        load_source(copies)

    depth = panels[0].shape[1]
    groups, _, rows, width = source.shape
    for q in range(per_step):
        tile = order[0, step * per_step + q]
        part = pick_product(
            source,
            [columns[tile, k] for k in range(depth)],
            [panels[q][0, k] for k in range(depth)],
        )
        solved = solve_block(rhs[q][...].reshape(part.shape), part, inverse[q][0])
        out[0, :, :, q * width : (q + 1) * width] = solved.reshape(groups, rows, width)


def leaf_solve(root, level, rhs, panels, inverse, order, columns, peers):
    subs, groups, blocks, rows, width = root.shape
    tiles, depth = panels.shape[:2]
    per_step = tiles // peers
    level_blocks = level.shape[0]
    rhs = rhs.reshape(groups, rows, tiles * width)

    def tile_of(q):
        return lambda i, order, columns: order[0, i * per_step + q]

    def spec(shape, index):
        return [
            pl.BlockSpec(shape, functools.partial(index, q)) for q in range(per_step)
        ]

    def rhs_index(q, i, order, columns):
        return (0, 0, order[0, i * per_step + q])

    def panel_index(q, i, order, columns):
        return (order[0, i * per_step + q], 0, 0, 0)

    def inverse_index(q, i, order, columns):
        return (order[0, i * per_step + q], 0, 0)

    return pl.pallas_call(
        functools.partial(leaf_kernel, per_step),
        out_shape=jax.ShapeDtypeStruct(
            (peers, groups, rows, per_step * width), jnp.bfloat16
        ),
        grid_spec=pltpu.PrefetchScalarGridSpec(
            num_scalar_prefetch=2,
            grid=(peers,),
            in_specs=[pl.BlockSpec(memory_space=pl.ANY)] * 2
            + spec((groups, rows, width), rhs_index)
            + spec((1, depth, width, width), panel_index)
            + spec((1, width, width), inverse_index),
            out_specs=pl.BlockSpec(
                (1, groups, rows, per_step * width),
                lambda i, order, columns: (i, 0, 0, 0),
            ),
            scratch_shapes=[
                pltpu.VMEM(
                    (groups, subs * blocks + level_blocks, rows, width), jnp.bfloat16
                ),
                pltpu.SemaphoreType.DMA((subs * groups + level_blocks,)),
            ],
        ),
        compiler_params=pltpu.CompilerParams(vmem_limit_bytes=48 * 2**20),
        name="leaf_solve",
    )(
        order,
        columns,
        root,
        level,
        *([rhs] * per_step),
        *([panels] * per_step),
        *([inverse] * per_step),
    )


def on_device(
    root_rhs,
    root_inverse,
    level_rhs,
    level_inverse,
    level_panels,
    level_columns,
    leaf_rhs,
    leaf_inverse,
    leaf_panels,
    leaf_columns,
    slab_order,
):
    width = leaf_panels.shape[2]
    subs, peers = lax.axis_size("sub"), lax.axis_size("dev")
    row_count = leaf_rhs.shape[0]
    piece_rows = root_rhs.shape[0]
    blocks = root_inverse.shape[0]
    piece = jnp.einsum(
        "rnj,nij->nri",
        root_rhs.reshape(piece_rows, blocks, width),
        root_inverse,
        preferred_element_type=jnp.float32,
    ).astype(jnp.bfloat16)
    root = lax.all_gather(piece, ("sub", "dev"), axis=0, tiled=False)
    root = root.reshape(subs, peers, blocks, piece_rows, width)
    if piece_rows % 16:
        root = root.transpose(0, 2, 1, 3, 4).reshape(subs, 1, blocks, row_count, width)
    level = level_solve(root, level_rhs, level_panels, level_inverse, level_columns)
    level = lax.all_gather(level, "dev", axis=0, tiled=False)
    outgoing = leaf_solve(
        root, level, leaf_rhs, leaf_panels, leaf_inverse, slab_order, leaf_columns, peers
    )
    outgoing = outgoing.reshape(peers, row_count, -1)
    arrived = lax.all_to_all(outgoing, "dev", split_axis=0, concat_axis=0, tiled=True)
    return arrived.transpose(1, 0, 2).reshape(row_count, -1)


def solution(mesh):
    in_specs = (
        P("dev", "sub"),
        P("sub", None, None),
        P(None, ("sub", "dev")),
        P(("sub", "dev"), None, None),
        P(("sub", "dev"), None, None, None),
        P(("sub", "dev"), None),
        P(None, ("sub", "dev")),
        P(("sub", "dev"), None, None),
        P(("sub", "dev"), None, None, None),
        P(("sub", "dev"), None),
        P(("sub", "dev"), None),
    )
    out_specs = P(None, ("sub", "dev"))
    return jax.shard_map(
        on_device, mesh=mesh, in_specs=in_specs, out_specs=out_specs, check_vma=False
    )
```

```python
import functools

import jax
import jax.numpy as jnp
from jax import lax
from jax.experimental import pallas as pl
from jax.experimental.pallas import tpu as pltpu
from jax.sharding import PartitionSpec as P

NT = (((1,), (1,)), ((), ()))
ANY = pl.BlockSpec(memory_space=pltpu.HBM)
SMEM = pl.BlockSpec(memory_space=pltpu.SMEM)
VMEM_LIMIT = 60 * 2**20
SMALL = pl.CostEstimate(flops=1000, bytes_accessed=1000, transcendentals=0)


def pick_product(source, columns, panels):
    groups, _, rows, width = source.shape
    picked = [source[:, col].reshape(groups * rows, width) for col in columns]
    total = None
    step = 2 if len(picked) % 2 == 0 else 1
    for k in range(0, len(picked), step):
        left = jnp.concatenate(picked[k : k + step], axis=1)
        right = jnp.concatenate(panels[k : k + step], axis=1)
        term = lax.dot_general(left, right, NT, preferred_element_type=jnp.float32)
        total = term if total is None else total + term
    return total


def solve_block(rhs, part, inverse):
    residue = (rhs.astype(jnp.float32) - part).astype(jnp.bfloat16)
    return lax.dot_general(
        residue, inverse, NT, preferred_element_type=jnp.float32
    ).astype(jnp.bfloat16)


def run_copies(pairs, sems):
    copies = [
        pltpu.make_async_copy(src, dst, sems.at[i]) for i, (src, dst) in enumerate(pairs)
    ]
    for copy in copies:
        copy.start()
    for copy in copies:
        copy.wait()


def flat_permute(value, dx=0, dz=0, dy=0, dc=0):
    step = dx * 16 + dz * 4 + dy * 2 + dc
    return lax.ppermute(value, ("sub", "dev"), [(i, i ^ step) for i in range(32)])


def after(values, event):
    return lax.optimization_barrier((values, event))[0]


SIDES = ((0, 0), (1, 0), (0, 1), (1, 1))


def gather_root(piece):
    found = {}

    def plane(dz, base):
        found[0, dz, 0, 0] = base
        for dx, dy in SIDES[1:]:
            found[dx, dz, dy, 0] = flat_permute(base, dx=dx, dy=dy)
        return [found[dx, dz, dy, 0] for dx, dy in SIDES]

    def chip(dz):
        for dx, dy in SIDES:
            found[dx, dz, dy, 1] = flat_permute(found[dx, dz, dy, 0], dc=1)

    near = flat_permute(piece, dz=1)
    far = flat_permute(piece, dz=2)
    own_plane = plane(0, piece)
    last = flat_permute(after(piece, near), dz=3)
    near_plane = plane(1, after(near, own_plane))
    chip(0)
    plane(2, after(far, own_plane))
    chip(1)
    plane(3, after(last, near_plane))
    chip(2)
    chip(3)
    return found


def piece_pairs(keys, pieces, source, groups):
    me_sub, me_dev = lax.axis_index("sub"), lax.axis_index("dev")
    pairs = []
    for (dx, dz, dy, dc), piece in zip(keys, pieces):
        blocks = piece.shape[0]
        group = (me_dev ^ (dz * 4 + dy * 2 + dc)) % groups
        pairs.append((piece, source.at[group, pl.ds((me_sub ^ dx) * blocks, blocks)]))
    return pairs


def level_kernel(keys, columns, *refs):
    count = len(keys)
    pieces = refs[:count]
    rhs, panels, inverse, out, source, sems = refs[count:]
    run_copies(piece_pairs(keys, pieces, source, source.shape[0]), sems)
    tiles = panels.shape[1]
    part = pick_product(
        source,
        [columns[0, k] for k in range(tiles)],
        [panels[0, k] for k in range(tiles)],
    )
    solved = solve_block(rhs[...], part, inverse[0])
    out[...] = solved.reshape(out.shape)


def level_block(found, rhs, panels, inverse, columns):
    keys = tuple(sorted(found))
    pieces = [found[key] for key in keys]
    blocks, rows, width = pieces[0].shape
    vmem = pl.BlockSpec(memory_space=pltpu.VMEM)
    return pl.pallas_call(
        functools.partial(level_kernel, keys),
        out_shape=jax.ShapeDtypeStruct((16, rows, width), jnp.bfloat16),
        in_specs=[SMEM] + [ANY] * len(keys) + [vmem] * 3,
        out_specs=vmem,
        scratch_shapes=[
            pltpu.VMEM((16, 2 * blocks, rows, width), jnp.bfloat16),
            pltpu.SemaphoreType.DMA((len(keys),)),
        ],
        compiler_params=pltpu.CompilerParams(vmem_limit_bytes=VMEM_LIMIT),
        cost_estimate=SMALL,
        name="level_block",
    )(columns, *pieces, rhs, panels, inverse)


def swap_cores(value):
    return lax.ppermute(value, "dev", [(i, i ^ 1) for i in range(16)])


def stack_kernel(*refs):
    for i, ref in enumerate(refs[:-1]):
        refs[-1][i] = ref[...]


def gather_level(block):
    found = [block]
    for k in range(2, 16, 2):
        found.append(lax.ppermute(block, "dev", [(i, i ^ k) for i in range(16)]))
    vmem = pl.BlockSpec(memory_space=pltpu.VMEM)
    mine = pl.pallas_call(
        stack_kernel,
        out_shape=jax.ShapeDtypeStruct((8,) + block.shape, block.dtype),
        in_specs=[vmem] * 8,
        out_specs=vmem,
        cost_estimate=SMALL,
        name="stack_level",
    )(*found)
    return mine, swap_cores(mine)


def leaf_kernel(part_index, keys, order, columns, *refs):
    count = len(keys)
    pieces = refs[:count]
    level, sibling, rhs_hbm, inverse_hbm, panels_hbm = refs[count : count + 5]
    out, source, rhs, inverse, panels, solved, sems, panel_sems, out_sems = refs[
        count + 5 :
    ]
    steps = out.shape[0]
    me_dev = lax.axis_index("dev")
    chip, core = me_dev // 2, me_dev % 2
    first = source.shape[1] - steps

    def tile_at(step, q):
        return order[0, step * 4 + q]

    def panel_copy(step, q):
        spot = step * 4 + q
        return pltpu.make_async_copy(
            panels_hbm.at[tile_at(step, q)], panels.at[spot], panel_sems.at[spot]
        )

    groups, _, rows, width = source.shape
    half = (me_dev // groups) ^ part_index
    mine = pl.ds(half * groups, groups)
    pairs = piece_pairs(keys, pieces, source, groups)
    for i in range(level.shape[0]):
        owner = first + (chip ^ i) * 2
        pairs.append((level.at[i, mine], source.at[:, owner + core]))
        pairs.append((sibling.at[i, mine], source.at[:, owner + 1 - core]))
    pairs.append((rhs_hbm.at[half], rhs))
    pairs.append((inverse_hbm, inverse))
    copies = [
        pltpu.make_async_copy(src, dst, sems.at[i]) for i, (src, dst) in enumerate(pairs)
    ]
    for copy in copies:
        copy.start()

    @pl.loop(0, steps)
    def _(step):
        for q in range(4):
            panel_copy(step, q).start()

    for copy in copies:
        copy.wait()

    depth = panels.shape[1]

    @pl.loop(0, steps)
    def _(step):
        slot = lax.rem(step, 2)

        @pl.when(step >= 2)
        def _():
            pltpu.make_async_copy(
                solved.at[slot], out.at[step], out_sems.at[slot]
            ).wait()

        for q in range(4):
            panel_copy(step, q).wait()
        tiles = [tile_at(step, q) for q in range(4)]
        parts = [
            pick_product(
                source,
                [columns[tile, k] for k in range(depth)],
                [panels[step * 4 + q, k] for k in range(depth)],
            )
            for q, tile in enumerate(tiles)
        ]
        for q, tile in enumerate(tiles):
            own = rhs[:, :, pl.ds(pl.multiple_of(tile * width, width), width)]
            done = solve_block(own.reshape(parts[q].shape), parts[q], inverse[tile])
            solved[slot, :, :, q * width : (q + 1) * width] = done.reshape(
                groups, rows, width
            )
        pltpu.make_async_copy(solved.at[slot], out.at[step], out_sems.at[slot]).start()

    for i in range(2):
        pltpu.make_async_copy(solved.at[i], out.at[i], out_sems.at[i]).wait()


def leaf_part(
    part_index, found, level, rhs, panels, inverse, order, columns
):
    keys = tuple(sorted(key for key in found if key[1] // 2 == part_index))
    pieces = [found[key] for key in keys]
    blocks, rows, width = pieces[0].shape
    groups = 8
    tiles, depth = panels.shape[:2]
    level_blocks = 16
    return pl.pallas_call(
        functools.partial(leaf_kernel, part_index, keys),
        out_shape=jax.ShapeDtypeStruct(
            (level_blocks, groups, rows, 4 * width), jnp.bfloat16
        ),
        in_specs=[SMEM] * 2 + [ANY] * (len(keys) + 5),
        out_specs=ANY,
        scratch_shapes=[
            pltpu.VMEM((groups, 2 * blocks + level_blocks, rows, width), jnp.bfloat16),
            pltpu.VMEM((groups, rows, tiles * width), jnp.bfloat16),
            pltpu.VMEM((tiles, width, width), jnp.bfloat16),
            pltpu.VMEM((tiles, depth, width, width), jnp.bfloat16),
            pltpu.VMEM((2, groups, rows, 4 * width), jnp.bfloat16),
            pltpu.SemaphoreType.DMA((len(keys) + level_blocks + 2,)),
            pltpu.SemaphoreType.DMA((tiles,)),
            pltpu.SemaphoreType.DMA((2,)),
        ],
        compiler_params=pltpu.CompilerParams(vmem_limit_bytes=VMEM_LIMIT),
        cost_estimate=SMALL,
        name="leaf_part",
    )(
        order,
        columns,
        *pieces,
        *level,
        rhs.reshape(2, groups, rows, tiles * width),
        inverse,
        panels,
    )


def place_kernel(part_index, arrived, *refs):
    out, held, in_sems, out_sems = refs[-4:]
    count, groups, _, span = arrived.shape
    inward = [
        pltpu.make_async_copy(arrived.at[k], held.at[k], in_sems.at[k])
        for k in range(count)
    ]
    for copy in inward:
        copy.start()
    outward = [
        pltpu.make_async_copy(
            held.at[k],
            out.at[(k // groups) ^ part_index, :, :, pl.ds(k * span, span)],
            out_sems.at[k],
        )
        for k in range(count)
    ]
    for k in range(count):
        inward[k].wait()
        outward[k].start()
    for copy in outward:
        copy.wait()


def place_part(part_index, arrived, before):
    count, groups, rows, span = arrived.shape
    extra = [] if before is None else [before]
    return pl.pallas_call(
        functools.partial(place_kernel, part_index),
        out_shape=jax.ShapeDtypeStruct((2, groups, rows, count * span), jnp.bfloat16),
        in_specs=[ANY] * (1 + len(extra)),
        out_specs=ANY,
        scratch_shapes=[
            pltpu.VMEM((count, groups, rows, span), jnp.bfloat16),
            pltpu.SemaphoreType.DMA((count,)),
            pltpu.SemaphoreType.DMA((count,)),
        ],
        input_output_aliases={} if before is None else {1: 0},
        compiler_params=pltpu.CompilerParams(vmem_limit_bytes=VMEM_LIMIT),
        cost_estimate=SMALL,
        name="place_part",
    )(arrived, *extra)


def on_device_pairs(
    root_rhs,
    root_inverse,
    level_rhs,
    level_inverse,
    level_panels,
    level_columns,
    leaf_rhs,
    leaf_inverse,
    leaf_panels,
    leaf_columns,
    slab_order,
):
    width = leaf_panels.shape[2]
    piece = jnp.einsum(
        "rnj,nij->nri",
        root_rhs.reshape(root_rhs.shape[0], root_inverse.shape[0], width),
        root_inverse,
        preferred_element_type=jnp.float32,
    ).astype(jnp.bfloat16)
    found = gather_root(piece)
    block = level_block(found, level_rhs, level_panels, level_inverse, level_columns)
    level = gather_level(block)

    def leaf_of(part_index):
        return leaf_part(
            part_index,
            found,
            level,
            leaf_rhs,
            leaf_panels,
            leaf_inverse,
            slab_order,
            leaf_columns,
        )

    def exchange(value):
        return lax.all_to_all(value, "dev", split_axis=0, concat_axis=0, tiled=True)

    out = None
    for part_index in range(2):
        out = place_part(part_index, exchange(leaf_of(part_index)), out)
    return out.reshape(leaf_rhs.shape)


def load_source(copies):
    for copy in copies:
        copy.start()
    for copy in copies:
        copy.wait()


def level_kernel_any(columns, root_hbm, rhs, panels, inverse, out, source, sems):
    subs, groups, blocks = root_hbm.shape[:3]
    copies = []
    for s in range(subs):
        for e in range(groups):
            copies.append(
                pltpu.make_async_copy(
                    root_hbm.at[s, e],
                    source.at[e, pl.ds(s * blocks, blocks)],
                    sems.at[s * groups + e],
                )
            )
    load_source(copies)
    tiles = panels.shape[1]
    part = pick_product(
        source,
        [columns[0, k] for k in range(tiles)],
        [panels[0, k] for k in range(tiles)],
    )
    shape = rhs.shape
    solved = solve_block(rhs[...].reshape(part.shape), part, inverse[0])
    out[...] = solved.reshape(shape)


def level_solve(root, rhs, panels, inverse, columns):
    subs, groups, blocks, rows, width = root.shape
    vmem = pl.BlockSpec(memory_space=pltpu.VMEM)
    return pl.pallas_call(
        level_kernel_any,
        out_shape=jax.ShapeDtypeStruct((groups, rows, width), jnp.bfloat16),
        in_specs=[
            pl.BlockSpec(memory_space=pltpu.SMEM),
            pl.BlockSpec(memory_space=pl.ANY),
            vmem,
            vmem,
            vmem,
        ],
        out_specs=vmem,
        scratch_shapes=[
            pltpu.VMEM((groups, subs * blocks, rows, width), jnp.bfloat16),
            pltpu.SemaphoreType.DMA((subs * groups,)),
        ],
        compiler_params=pltpu.CompilerParams(vmem_limit_bytes=40 * 2**20),
        name="level_solve",
    )(columns, root, rhs.reshape(groups, rows, width), panels, inverse)


def leaf_kernel_any(per_step, order, columns, root_hbm, level_hbm, *refs):
    rhs = refs[:per_step]
    panels = refs[per_step : 2 * per_step]
    inverse = refs[2 * per_step : 3 * per_step]
    out, source, sems = refs[3 * per_step :]
    subs, groups, blocks = root_hbm.shape[:3]
    level_blocks = level_hbm.shape[0]
    step = pl.program_id(0)

    @pl.when(step == 0)
    def _():
        copies = []
        for s in range(subs):
            for e in range(groups):
                copies.append(
                    pltpu.make_async_copy(
                        root_hbm.at[s, e],
                        source.at[e, pl.ds(s * blocks, blocks)],
                        sems.at[s * groups + e],
                    )
                )
        for j in range(level_blocks):
            copies.append(
                pltpu.make_async_copy(
                    level_hbm.at[j],
                    source.at[:, subs * blocks + j],
                    sems.at[subs * groups + j],
                )
            )
        load_source(copies)

    depth = panels[0].shape[1]
    groups, _, rows, width = source.shape
    for q in range(per_step):
        tile = order[0, step * per_step + q]
        part = pick_product(
            source,
            [columns[tile, k] for k in range(depth)],
            [panels[q][0, k] for k in range(depth)],
        )
        solved = solve_block(rhs[q][...].reshape(part.shape), part, inverse[q][0])
        out[0, :, :, q * width : (q + 1) * width] = solved.reshape(groups, rows, width)


def leaf_solve(root, level, rhs, panels, inverse, order, columns, peers):
    subs, groups, blocks, rows, width = root.shape
    tiles, depth = panels.shape[:2]
    per_step = tiles // peers
    level_blocks = level.shape[0]
    rhs = rhs.reshape(groups, rows, tiles * width)

    def tile_of(q):
        return lambda i, order, columns: order[0, i * per_step + q]

    def spec(shape, index):
        return [
            pl.BlockSpec(shape, functools.partial(index, q)) for q in range(per_step)
        ]

    def rhs_index(q, i, order, columns):
        return (0, 0, order[0, i * per_step + q])

    def panel_index(q, i, order, columns):
        return (order[0, i * per_step + q], 0, 0, 0)

    def inverse_index(q, i, order, columns):
        return (order[0, i * per_step + q], 0, 0)

    return pl.pallas_call(
        functools.partial(leaf_kernel_any, per_step),
        out_shape=jax.ShapeDtypeStruct(
            (peers, groups, rows, per_step * width), jnp.bfloat16
        ),
        grid_spec=pltpu.PrefetchScalarGridSpec(
            num_scalar_prefetch=2,
            grid=(peers,),
            in_specs=[pl.BlockSpec(memory_space=pl.ANY)] * 2
            + spec((groups, rows, width), rhs_index)
            + spec((1, depth, width, width), panel_index)
            + spec((1, width, width), inverse_index),
            out_specs=pl.BlockSpec(
                (1, groups, rows, per_step * width),
                lambda i, order, columns: (i, 0, 0, 0),
            ),
            scratch_shapes=[
                pltpu.VMEM(
                    (groups, subs * blocks + level_blocks, rows, width), jnp.bfloat16
                ),
                pltpu.SemaphoreType.DMA((subs * groups + level_blocks,)),
            ],
        ),
        compiler_params=pltpu.CompilerParams(vmem_limit_bytes=48 * 2**20),
        name="leaf_solve",
    )(
        order,
        columns,
        root,
        level,
        *([rhs] * per_step),
        *([panels] * per_step),
        *([inverse] * per_step),
    )


def on_device_any(
    root_rhs,
    root_inverse,
    level_rhs,
    level_inverse,
    level_panels,
    level_columns,
    leaf_rhs,
    leaf_inverse,
    leaf_panels,
    leaf_columns,
    slab_order,
):
    width = leaf_panels.shape[2]
    subs, peers = lax.axis_size("sub"), lax.axis_size("dev")
    row_count = leaf_rhs.shape[0]
    piece_rows = root_rhs.shape[0]
    blocks = root_inverse.shape[0]
    piece = jnp.einsum(
        "rnj,nij->nri",
        root_rhs.reshape(piece_rows, blocks, width),
        root_inverse,
        preferred_element_type=jnp.float32,
    ).astype(jnp.bfloat16)
    root = lax.all_gather(piece, ("sub", "dev"), axis=0, tiled=False)
    root = root.reshape(subs, peers, blocks, piece_rows, width)
    if piece_rows % 16:
        root = root.transpose(0, 2, 1, 3, 4).reshape(subs, 1, blocks, row_count, width)
    level = level_solve(root, level_rhs, level_panels, level_inverse, level_columns)
    level = lax.all_gather(level, "dev", axis=0, tiled=False)
    outgoing = leaf_solve(
        root, level, leaf_rhs, leaf_panels, leaf_inverse, slab_order, leaf_columns, peers
    )
    outgoing = outgoing.reshape(peers, row_count, -1)
    arrived = lax.all_to_all(outgoing, "dev", split_axis=0, concat_axis=0, tiled=True)
    return arrived.transpose(1, 0, 2).reshape(row_count, -1)


def solution(mesh):
    in_specs = (
        P("dev", "sub"),
        P("sub", None, None),
        P(None, ("sub", "dev")),
        P(("sub", "dev"), None, None),
        P(("sub", "dev"), None, None, None),
        P(("sub", "dev"), None),
        P(None, ("sub", "dev")),
        P(("sub", "dev"), None, None),
        P(("sub", "dev"), None, None, None),
        P(("sub", "dev"), None),
        P(("sub", "dev"), None),
    )
    out_specs = P(None, ("sub", "dev"))
    fits = mesh.shape["sub"] == 2 and mesh.shape["dev"] == 16
    on_device = on_device_pairs if fits else on_device_any
    return jax.shard_map(
        on_device, mesh=mesh, in_specs=in_specs, out_specs=out_specs, check_vma=False
    )
```

```python
import functools

import jax
import jax.numpy as jnp
from jax import lax
from jax.experimental import pallas as pl
from jax.experimental.pallas import tpu as pltpu
from jax.sharding import PartitionSpec as P

NT = (((1,), (1,)), ((), ()))
ANY = pl.BlockSpec(memory_space=pltpu.HBM)
SMEM = pl.BlockSpec(memory_space=pltpu.SMEM)
VMEM_LIMIT = 60 * 2**20
TOGETHER = 2
SMALL = pl.CostEstimate(flops=1000, bytes_accessed=1000, transcendentals=0)


def pick_product(source, columns, panels):
    groups, _, rows, width = source.shape
    picked = [source[:, col].reshape(groups * rows, width) for col in columns]
    total = None
    step = 2 if len(picked) % 2 == 0 else 1
    for k in range(0, len(picked), step):
        left = jnp.concatenate(picked[k : k + step], axis=1)
        right = jnp.concatenate(panels[k : k + step], axis=1)
        term = lax.dot_general(left, right, NT, preferred_element_type=jnp.float32)
        total = term if total is None else total + term
    return total


def solve_block(rhs, part, inverse):
    residue = (rhs.astype(jnp.float32) - part).astype(jnp.bfloat16)
    return lax.dot_general(
        residue, inverse, NT, preferred_element_type=jnp.float32
    ).astype(jnp.bfloat16)


def run_copies(pairs, sems):
    copies = [
        pltpu.make_async_copy(src, dst, sems.at[i]) for i, (src, dst) in enumerate(pairs)
    ]
    for copy in copies:
        copy.start()
    for copy in copies:
        copy.wait()


def flat_permute(value, dx=0, dz=0, dy=0, dc=0):
    step = dx * 16 + dz * 4 + dy * 2 + dc
    return lax.ppermute(value, ("sub", "dev"), [(i, i ^ step) for i in range(32)])


def after(values, event):
    return lax.optimization_barrier((values, event))[0]


SIDES = ((0, 0), (1, 0), (0, 1), (1, 1))


def gather_root(piece):
    found = {}

    def plane(dz, base, x_first):
        from_x = flat_permute(base, dx=1)
        from_y = flat_permute(base, dy=1)
        if x_first:
            corner = flat_permute(from_x, dy=1)
        else:
            corner = flat_permute(from_y, dx=1)
        for (dx, dy), value in zip(SIDES, (base, from_x, from_y, corner)):
            found[dx, dz, dy, 0] = value
        return from_x, from_y

    near = flat_permute(piece, dz=1)
    far = flat_permute(piece, dz=2)
    sides = plane(0, piece, True)
    last = flat_permute(after(piece, far), dz=3)
    sides = plane(1, after(near, sides), False)
    sides = plane(2, after(far, sides), True)
    plane(3, after(last, sides), False)
    for key in tuple(found):
        found[key[:3] + (1,)] = flat_permute(found[key], dc=1)
    return found


def piece_pairs(keys, pieces, source, groups):
    me_sub, me_dev = lax.axis_index("sub"), lax.axis_index("dev")
    pairs = []
    for (dx, dz, dy, dc), piece in zip(keys, pieces):
        blocks = piece.shape[0]
        group = (me_dev ^ (dz * 4 + dy * 2 + dc)) % groups
        pairs.append((piece, source.at[group, pl.ds((me_sub ^ dx) * blocks, blocks)]))
    return pairs


def level_kernel(keys, columns, *refs):
    count = len(keys)
    pieces = refs[:count]
    rhs, panels, inverse, out, source, sems = refs[count:]
    run_copies(piece_pairs(keys, pieces, source, source.shape[0]), sems)
    tiles = panels.shape[1]
    part = pick_product(
        source,
        [columns[0, k] for k in range(tiles)],
        [panels[0, k] for k in range(tiles)],
    )
    solved = solve_block(rhs[...], part, inverse[0])
    out[...] = solved.reshape(out.shape)


def level_block(found, rhs, panels, inverse, columns):
    keys = tuple(sorted(found))
    pieces = [found[key] for key in keys]
    blocks, rows, width = pieces[0].shape
    vmem = pl.BlockSpec(memory_space=pltpu.VMEM)
    return pl.pallas_call(
        functools.partial(level_kernel, keys),
        out_shape=jax.ShapeDtypeStruct((16, rows, width), jnp.bfloat16),
        in_specs=[SMEM] + [ANY] * len(keys) + [vmem] * 3,
        out_specs=vmem,
        scratch_shapes=[
            pltpu.VMEM((16, 2 * blocks, rows, width), jnp.bfloat16),
            pltpu.SemaphoreType.DMA((len(keys),)),
        ],
        compiler_params=pltpu.CompilerParams(vmem_limit_bytes=VMEM_LIMIT),
        cost_estimate=SMALL,
        name="level_block",
    )(columns, *pieces, rhs, panels, inverse)


def swap_cores(value):
    return lax.ppermute(value, "dev", [(i, i ^ 1) for i in range(16)])


def stack_kernel(*refs):
    for i, ref in enumerate(refs[:-1]):
        refs[-1][i] = ref[...]


def gather_level(block):
    found = [block]
    for k in range(2, 16, 2):
        found.append(lax.ppermute(block, "dev", [(i, i ^ k) for i in range(16)]))
    vmem = pl.BlockSpec(memory_space=pltpu.VMEM)
    mine = pl.pallas_call(
        stack_kernel,
        out_shape=jax.ShapeDtypeStruct((8,) + block.shape, block.dtype),
        in_specs=[vmem] * 8,
        out_specs=vmem,
        cost_estimate=SMALL,
        name="stack_level",
    )(*found)
    return mine, swap_cores(mine)


def leaf_kernel(part_index, keys, order, columns, *refs):
    count = len(keys)
    pieces = refs[:count]
    level, sibling, rhs_hbm, inverse_hbm, panels_hbm = refs[count : count + 5]
    out, source, rhs, inverse, panels, solved, sems, tile_sems, out_sems = refs[
        count + 5 :
    ]
    steps = out.shape[0]
    me_dev = lax.axis_index("dev")
    chip, core = me_dev // 2, me_dev % 2
    first = source.shape[1] - steps

    def tile_at(step, q):
        return order[0, step * 4 + q]

    groups, _, rows, width = source.shape
    half = (me_dev // groups) ^ part_index
    mine = pl.ds(half * groups, groups)
    pairs = piece_pairs(keys, pieces, source, groups)
    for i in range(level.shape[0]):
        owner = first + (chip ^ i) * 2
        pairs.append((level.at[i, mine], source.at[:, owner + core]))
        pairs.append((sibling.at[i, mine], source.at[:, owner + 1 - core]))

    def panel_copy(step, q):
        spot = step * 4 + q
        return pltpu.make_async_copy(
            panels_hbm.at[tile_at(step, q)], panels.at[spot], tile_sems.at[spot]
        )

    copies = [
        pltpu.make_async_copy(src, dst, sems.at[i]) for i, (src, dst) in enumerate(pairs)
    ]
    for copy in copies:
        copy.start()

    for step in range(TOGETHER):
        for q in range(4):
            panel_copy(step, q).start()
    shared = [
        pltpu.make_async_copy(rhs_hbm.at[half], rhs, sems.at[len(pairs)]),
        pltpu.make_async_copy(inverse_hbm, inverse, sems.at[len(pairs) + 1]),
    ]
    for copy in shared:
        copy.start()

    @pl.loop(TOGETHER, steps)
    def _(step):
        for q in range(4):
            panel_copy(step, q).start()

    for copy in copies + shared:
        copy.wait()

    depth = panels.shape[1]

    @pl.loop(0, steps // TOGETHER)
    def _(turn):
        slot = lax.rem(turn, 2)
        spots = [(turn * TOGETHER + i, q) for i in range(TOGETHER) for q in range(4)]

        def out_copy(turn):
            return pltpu.make_async_copy(
                solved.at[slot],
                out.at[pl.ds(turn * TOGETHER, TOGETHER)],
                out_sems.at[slot],
            )

        @pl.when(turn >= 2)
        def _():
            out_copy(turn).wait()

        for step, q in spots:
            panel_copy(step, q).wait()
        parts = []
        for step, q in spots:
            tile = tile_at(step, q)
            parts.append(
                pick_product(
                    source,
                    [columns[0, tile * depth + k] for k in range(depth)],
                    [panels[step * 4 + q, k] for k in range(depth)],
                )
            )
        for i, ((step, q), part) in enumerate(zip(spots, parts)):
            tile = tile_at(step, q)
            lanes = pl.ds(pl.multiple_of(tile * width, width), width)
            own = rhs[:, :, lanes].reshape(part.shape)
            done = solve_block(own, part, inverse[tile])
            solved[slot, i // 4, :, :, q * width : (q + 1) * width] = done.reshape(
                groups, rows, width
            )
        out_copy(turn).start()

    for i in range(2):
        pltpu.make_async_copy(
            solved.at[i], out.at[pl.ds(i * TOGETHER, TOGETHER)], out_sems.at[i]
        ).wait()


def leaf_part(
    part_index, found, level, rhs, panels, inverse, order, columns
):
    keys = tuple(sorted(key for key in found if key[1] // 2 == part_index))
    pieces = [found[key] for key in keys]
    blocks, rows, width = pieces[0].shape
    groups = 8
    tiles, depth = panels.shape[:2]
    level_blocks = 16
    return pl.pallas_call(
        functools.partial(leaf_kernel, part_index, keys),
        out_shape=jax.ShapeDtypeStruct(
            (level_blocks, groups, rows, 4 * width), jnp.bfloat16
        ),
        in_specs=[SMEM] * 2 + [ANY] * (len(keys) + 5),
        out_specs=ANY,
        scratch_shapes=[
            pltpu.VMEM((groups, 2 * blocks + level_blocks, rows, width), jnp.bfloat16),
            pltpu.VMEM((groups, rows, tiles * width), jnp.bfloat16),
            pltpu.VMEM((tiles, width, width), jnp.bfloat16),
            pltpu.VMEM((tiles, depth, width, width), jnp.bfloat16),
            pltpu.VMEM((2, TOGETHER, groups, rows, 4 * width), jnp.bfloat16),
            pltpu.SemaphoreType.DMA((len(keys) + level_blocks + 2,)),
            pltpu.SemaphoreType.DMA((tiles,)),
            pltpu.SemaphoreType.DMA((2,)),
        ],
        compiler_params=pltpu.CompilerParams(vmem_limit_bytes=VMEM_LIMIT),
        cost_estimate=SMALL,
        name="leaf_part",
    )(
        order,
        columns,
        *pieces,
        *level,
        rhs.reshape(2, groups, rows, tiles * width),
        inverse,
        panels,
    )


def place_kernel(part_index, arrived, *refs):
    out, held, in_sems, out_sems = refs[-4:]
    count, groups, _, span = arrived.shape
    inward = [
        pltpu.make_async_copy(arrived.at[k], held.at[k], in_sems.at[k])
        for k in range(count)
    ]
    for copy in inward:
        copy.start()
    outward = [
        pltpu.make_async_copy(
            held.at[k],
            out.at[(k // groups) ^ part_index, :, :, pl.ds(k * span, span)],
            out_sems.at[k],
        )
        for k in range(count)
    ]
    for k in range(count):
        inward[k].wait()
        outward[k].start()
    for copy in outward:
        copy.wait()


def place_part(part_index, arrived, before):
    count, groups, rows, span = arrived.shape
    extra = [] if before is None else [before]
    return pl.pallas_call(
        functools.partial(place_kernel, part_index),
        out_shape=jax.ShapeDtypeStruct((2, groups, rows, count * span), jnp.bfloat16),
        in_specs=[ANY] * (1 + len(extra)),
        out_specs=ANY,
        scratch_shapes=[
            pltpu.VMEM((count, groups, rows, span), jnp.bfloat16),
            pltpu.SemaphoreType.DMA((count,)),
            pltpu.SemaphoreType.DMA((count,)),
        ],
        input_output_aliases={} if before is None else {1: 0},
        compiler_params=pltpu.CompilerParams(vmem_limit_bytes=VMEM_LIMIT),
        cost_estimate=SMALL,
        name="place_part",
    )(arrived, *extra)


def on_device_pairs(
    root_rhs,
    root_inverse,
    level_rhs,
    level_inverse,
    level_panels,
    level_columns,
    leaf_rhs,
    leaf_inverse,
    leaf_panels,
    leaf_columns,
    slab_order,
):
    width = leaf_panels.shape[2]
    piece = jnp.einsum(
        "rnj,nij->nri",
        root_rhs.reshape(root_rhs.shape[0], root_inverse.shape[0], width),
        root_inverse,
        preferred_element_type=jnp.float32,
    ).astype(jnp.bfloat16)
    leaf_columns = leaf_columns.reshape(1, -1)
    found = gather_root(after(piece, leaf_columns))
    block = level_block(found, level_rhs, level_panels, level_inverse, level_columns)
    level = gather_level(block)

    def leaf_of(part_index):
        return leaf_part(
            part_index,
            found,
            level,
            leaf_rhs,
            leaf_panels,
            leaf_inverse,
            slab_order,
            leaf_columns,
        )

    def exchange(value):
        return lax.all_to_all(value, "dev", split_axis=0, concat_axis=0, tiled=True)

    out = None
    for part_index in range(2):
        out = place_part(part_index, exchange(leaf_of(part_index)), out)
    return out.reshape(leaf_rhs.shape)


def load_source(copies):
    for copy in copies:
        copy.start()
    for copy in copies:
        copy.wait()


def level_kernel_any(columns, root_hbm, rhs, panels, inverse, out, source, sems):
    subs, groups, blocks = root_hbm.shape[:3]
    copies = []
    for s in range(subs):
        for e in range(groups):
            copies.append(
                pltpu.make_async_copy(
                    root_hbm.at[s, e],
                    source.at[e, pl.ds(s * blocks, blocks)],
                    sems.at[s * groups + e],
                )
            )
    load_source(copies)
    tiles = panels.shape[1]
    part = pick_product(
        source,
        [columns[0, k] for k in range(tiles)],
        [panels[0, k] for k in range(tiles)],
    )
    shape = rhs.shape
    solved = solve_block(rhs[...].reshape(part.shape), part, inverse[0])
    out[...] = solved.reshape(shape)


def level_solve(root, rhs, panels, inverse, columns):
    subs, groups, blocks, rows, width = root.shape
    vmem = pl.BlockSpec(memory_space=pltpu.VMEM)
    return pl.pallas_call(
        level_kernel_any,
        out_shape=jax.ShapeDtypeStruct((groups, rows, width), jnp.bfloat16),
        in_specs=[
            pl.BlockSpec(memory_space=pltpu.SMEM),
            pl.BlockSpec(memory_space=pl.ANY),
            vmem,
            vmem,
            vmem,
        ],
        out_specs=vmem,
        scratch_shapes=[
            pltpu.VMEM((groups, subs * blocks, rows, width), jnp.bfloat16),
            pltpu.SemaphoreType.DMA((subs * groups,)),
        ],
        compiler_params=pltpu.CompilerParams(vmem_limit_bytes=40 * 2**20),
        name="level_solve",
    )(columns, root, rhs.reshape(groups, rows, width), panels, inverse)


def leaf_kernel_any(per_step, order, columns, root_hbm, level_hbm, *refs):
    rhs = refs[:per_step]
    panels = refs[per_step : 2 * per_step]
    inverse = refs[2 * per_step : 3 * per_step]
    out, source, sems = refs[3 * per_step :]
    subs, groups, blocks = root_hbm.shape[:3]
    level_blocks = level_hbm.shape[0]
    step = pl.program_id(0)

    @pl.when(step == 0)
    def _():
        copies = []
        for s in range(subs):
            for e in range(groups):
                copies.append(
                    pltpu.make_async_copy(
                        root_hbm.at[s, e],
                        source.at[e, pl.ds(s * blocks, blocks)],
                        sems.at[s * groups + e],
                    )
                )
        for j in range(level_blocks):
            copies.append(
                pltpu.make_async_copy(
                    level_hbm.at[j],
                    source.at[:, subs * blocks + j],
                    sems.at[subs * groups + j],
                )
            )
        load_source(copies)

    depth = panels[0].shape[1]
    groups, _, rows, width = source.shape
    for q in range(per_step):
        tile = order[0, step * per_step + q]
        part = pick_product(
            source,
            [columns[tile, k] for k in range(depth)],
            [panels[q][0, k] for k in range(depth)],
        )
        solved = solve_block(rhs[q][...].reshape(part.shape), part, inverse[q][0])
        out[0, :, :, q * width : (q + 1) * width] = solved.reshape(groups, rows, width)


def leaf_solve(root, level, rhs, panels, inverse, order, columns, peers):
    subs, groups, blocks, rows, width = root.shape
    tiles, depth = panels.shape[:2]
    per_step = tiles // peers
    level_blocks = level.shape[0]
    rhs = rhs.reshape(groups, rows, tiles * width)

    def tile_of(q):
        return lambda i, order, columns: order[0, i * per_step + q]

    def spec(shape, index):
        return [
            pl.BlockSpec(shape, functools.partial(index, q)) for q in range(per_step)
        ]

    def rhs_index(q, i, order, columns):
        return (0, 0, order[0, i * per_step + q])

    def panel_index(q, i, order, columns):
        return (order[0, i * per_step + q], 0, 0, 0)

    def inverse_index(q, i, order, columns):
        return (order[0, i * per_step + q], 0, 0)

    return pl.pallas_call(
        functools.partial(leaf_kernel_any, per_step),
        out_shape=jax.ShapeDtypeStruct(
            (peers, groups, rows, per_step * width), jnp.bfloat16
        ),
        grid_spec=pltpu.PrefetchScalarGridSpec(
            num_scalar_prefetch=2,
            grid=(peers,),
            in_specs=[pl.BlockSpec(memory_space=pl.ANY)] * 2
            + spec((groups, rows, width), rhs_index)
            + spec((1, depth, width, width), panel_index)
            + spec((1, width, width), inverse_index),
            out_specs=pl.BlockSpec(
                (1, groups, rows, per_step * width),
                lambda i, order, columns: (i, 0, 0, 0),
            ),
            scratch_shapes=[
                pltpu.VMEM(
                    (groups, subs * blocks + level_blocks, rows, width), jnp.bfloat16
                ),
                pltpu.SemaphoreType.DMA((subs * groups + level_blocks,)),
            ],
        ),
        compiler_params=pltpu.CompilerParams(vmem_limit_bytes=48 * 2**20),
        name="leaf_solve",
    )(
        order,
        columns,
        root,
        level,
        *([rhs] * per_step),
        *([panels] * per_step),
        *([inverse] * per_step),
    )


def on_device_any(
    root_rhs,
    root_inverse,
    level_rhs,
    level_inverse,
    level_panels,
    level_columns,
    leaf_rhs,
    leaf_inverse,
    leaf_panels,
    leaf_columns,
    slab_order,
):
    width = leaf_panels.shape[2]
    subs, peers = lax.axis_size("sub"), lax.axis_size("dev")
    row_count = leaf_rhs.shape[0]
    piece_rows = root_rhs.shape[0]
    blocks = root_inverse.shape[0]
    piece = jnp.einsum(
        "rnj,nij->nri",
        root_rhs.reshape(piece_rows, blocks, width),
        root_inverse,
        preferred_element_type=jnp.float32,
    ).astype(jnp.bfloat16)
    root = lax.all_gather(piece, ("sub", "dev"), axis=0, tiled=False)
    root = root.reshape(subs, peers, blocks, piece_rows, width)
    if piece_rows % 16:
        root = root.transpose(0, 2, 1, 3, 4).reshape(subs, 1, blocks, row_count, width)
    level = level_solve(root, level_rhs, level_panels, level_inverse, level_columns)
    level = lax.all_gather(level, "dev", axis=0, tiled=False)
    outgoing = leaf_solve(
        root, level, leaf_rhs, leaf_panels, leaf_inverse, slab_order, leaf_columns, peers
    )
    outgoing = outgoing.reshape(peers, row_count, -1)
    arrived = lax.all_to_all(outgoing, "dev", split_axis=0, concat_axis=0, tiled=True)
    return arrived.transpose(1, 0, 2).reshape(row_count, -1)


def solution(mesh):
    in_specs = (
        P("dev", "sub"),
        P("sub", None, None),
        P(None, ("sub", "dev")),
        P(("sub", "dev"), None, None),
        P(("sub", "dev"), None, None, None),
        P(("sub", "dev"), None),
        P(None, ("sub", "dev")),
        P(("sub", "dev"), None, None),
        P(("sub", "dev"), None, None, None),
        P(("sub", "dev"), None),
        P(("sub", "dev"), None),
    )
    out_specs = P(None, ("sub", "dev"))
    fits = mesh.shape["sub"] == 2 and mesh.shape["dev"] == 16
    on_device = on_device_pairs if fits else on_device_any
    return jax.shard_map(
        on_device, mesh=mesh, in_specs=in_specs, out_specs=out_specs, check_vma=False
    )
```

```python
import functools

import jax
import jax.numpy as jnp
from jax import lax
from jax.experimental import pallas as pl
from jax.experimental.pallas import tpu as pltpu
from jax.sharding import PartitionSpec as P

NT = (((1,), (1,)), ((), ()))
ANY = pl.BlockSpec(memory_space=pltpu.HBM)
SMEM = pl.BlockSpec(memory_space=pltpu.SMEM)
VMEM_LIMIT = 60 * 2**20
TOGETHER = 2
PARTS = ((0, 1), (2, 3))
SMALL = pl.CostEstimate(flops=1000, bytes_accessed=1000, transcendentals=0)


def pick_product(source, columns, panels):
    groups, _, rows, width = source.shape
    picked = [source[:, col].reshape(groups * rows, width) for col in columns]
    total = None
    step = 2 if len(picked) % 2 == 0 else 1
    for k in range(0, len(picked), step):
        left = jnp.concatenate(picked[k : k + step], axis=1)
        right = jnp.concatenate(panels[k : k + step], axis=1)
        term = lax.dot_general(left, right, NT, preferred_element_type=jnp.float32)
        total = term if total is None else total + term
    return total


def solve_block(rhs, part, inverse):
    residue = (rhs.astype(jnp.float32) - part).astype(jnp.bfloat16)
    return lax.dot_general(
        residue, inverse, NT, preferred_element_type=jnp.float32
    ).astype(jnp.bfloat16)


def run_copies(pairs, sems):
    copies = [
        pltpu.make_async_copy(src, dst, sems.at[i]) for i, (src, dst) in enumerate(pairs)
    ]
    for copy in copies:
        copy.start()
    for copy in copies:
        copy.wait()


def flat_permute(value, dx=0, dz=0, dy=0, dc=0):
    step = dx * 16 + dz * 4 + dy * 2 + dc
    return lax.ppermute(value, ("sub", "dev"), [(i, i ^ step) for i in range(32)])


def after(values, event):
    return lax.optimization_barrier((values, event))[0]


SIDES = ((0, 0), (1, 0), (0, 1), (1, 1))


def gather_root(piece):
    found = {}

    def plane(dz, base, x_first):
        from_x = flat_permute(base, dx=1)
        from_y = flat_permute(base, dy=1)
        if x_first:
            corner = flat_permute(from_x, dy=1)
        else:
            corner = flat_permute(from_y, dx=1)
        for (dx, dy), value in zip(SIDES, (base, from_x, from_y, corner)):
            found[dx, dz, dy, 0] = value
        return from_x, from_y

    near = flat_permute(piece, dz=1)
    far = flat_permute(piece, dz=2)
    sides = plane(0, piece, True)
    last = flat_permute(after(piece, sides), dz=3)
    sides = plane(1, after(near, sides), False)
    sides = plane(2, after(far, sides), True)
    plane(3, after(last, sides), False)
    for key in tuple(found):
        found[key[:3] + (1,)] = flat_permute(found[key], dc=1)
    return found


def piece_pairs(keys, pieces, source, groups):
    me_sub, me_dev = lax.axis_index("sub"), lax.axis_index("dev")
    pairs = []
    for (dx, dz, dy, dc), piece in zip(keys, pieces):
        blocks = piece.shape[0]
        group = (me_dev ^ (dz * 4 + dy * 2 + dc)) % groups
        pairs.append((piece, source.at[group, pl.ds((me_sub ^ dx) * blocks, blocks)]))
    return pairs


def level_kernel(keys, columns, *refs):
    count = len(keys)
    pieces = refs[:count]
    rhs, panels, inverse, out, source, sems = refs[count:]
    run_copies(piece_pairs(keys, pieces, source, source.shape[0]), sems)
    tiles = panels.shape[1]
    part = pick_product(
        source,
        [columns[0, k] for k in range(tiles)],
        [panels[0, k] for k in range(tiles)],
    )
    solved = solve_block(rhs[...], part, inverse[0])
    out[...] = solved.reshape(out.shape)


def level_block(found, rhs, panels, inverse, columns):
    keys = tuple(sorted(found, key=lambda key: key[1]))
    pieces = [found[key] for key in keys]
    blocks, rows, width = pieces[0].shape
    vmem = pl.BlockSpec(memory_space=pltpu.VMEM)
    return pl.pallas_call(
        functools.partial(level_kernel, keys),
        out_shape=jax.ShapeDtypeStruct((16, rows, width), jnp.bfloat16),
        in_specs=[SMEM] + [ANY] * len(keys) + [vmem] * 3,
        out_specs=vmem,
        scratch_shapes=[
            pltpu.VMEM((16, 2 * blocks, rows, width), jnp.bfloat16),
            pltpu.SemaphoreType.DMA((len(keys),)),
        ],
        compiler_params=pltpu.CompilerParams(vmem_limit_bytes=VMEM_LIMIT),
        cost_estimate=SMALL,
        name="level_block",
    )(columns, *pieces, rhs, panels, inverse)


def swap_cores(value):
    return lax.ppermute(value, "dev", [(i, i ^ 1) for i in range(16)])


def gather_level(block):
    mine = [block]
    for k in range(2, 16, 2):
        mine.append(lax.ppermute(block, "dev", [(i, i ^ k) for i in range(16)]))
    return mine + [swap_cores(value) for value in mine]


def leaf_kernel(part, keys, order, columns, *refs):
    count = len(keys)
    pieces = refs[:count]
    level = refs[count : count + 16]
    rhs_hbm, inverse_hbm, panels_hbm = refs[count + 16 : count + 19]
    out, source, rhs, inverse, panels, solved, sems, tile_sems, out_sems = refs[
        count + 19 :
    ]
    steps = out.shape[0]
    me_dev = lax.axis_index("dev")
    chip, core = me_dev // 2, me_dev % 2
    first = source.shape[1] - steps

    def tile_at(step, q):
        return order[0, step * 4 + q]

    groups, _, rows, width = source.shape
    z = me_dev // 4
    pairs = []
    for (dx, dz, dy, dc), piece in zip(keys, pieces):
        group = 4 * part.index(dz) + (me_dev ^ (2 * dy + dc)) % 4
        blocks = piece.shape[0]
        begin = (lax.axis_index("sub") ^ dx) * blocks
        pairs.append((piece, source.at[group, pl.ds(begin, blocks)]))
    for place, dz in enumerate(part):
        spot, mine = pl.ds(4 * place, 4), pl.ds((z ^ dz) * 4, 4)
        for i in range(8):
            owner = first + (chip ^ i) * 2
            pairs.append((level[i].at[mine], source.at[spot, owner + core]))
            pairs.append((level[8 + i].at[mine], source.at[spot, owner + 1 - core]))

    def panel_copy(step, q):
        spot = step * 4 + q
        return pltpu.make_async_copy(
            panels_hbm.at[tile_at(step, q)], panels.at[spot], tile_sems.at[spot]
        )

    copies = [
        pltpu.make_async_copy(src, dst, sems.at[i]) for i, (src, dst) in enumerate(pairs)
    ]
    for copy in copies:
        copy.start()

    for step in range(TOGETHER):
        for q in range(4):
            panel_copy(step, q).start()
    shared = [
        pltpu.make_async_copy(inverse_hbm, inverse, sems.at[len(pairs)]),
    ]
    shared += [
        pltpu.make_async_copy(
            rhs_hbm.at[z ^ dz], rhs.at[pl.ds(4 * i, 4)], sems.at[len(pairs) + 1 + i]
        )
        for i, dz in enumerate(part)
    ]
    for copy in shared:
        copy.start()

    @pl.loop(TOGETHER, steps)
    def _(step):
        for q in range(4):
            panel_copy(step, q).start()

    for copy in copies + shared:
        copy.wait()

    depth = panels.shape[1]

    @pl.loop(0, steps // TOGETHER)
    def _(turn):
        slot = lax.rem(turn, 2)
        spots = [(turn * TOGETHER + i, q) for i in range(TOGETHER) for q in range(4)]

        def out_copy(turn):
            return pltpu.make_async_copy(
                solved.at[slot],
                out.at[pl.ds(turn * TOGETHER, TOGETHER)],
                out_sems.at[slot],
            )

        @pl.when(turn >= 2)
        def _():
            out_copy(turn).wait()

        for step, q in spots:
            panel_copy(step, q).wait()
        sums = []
        for step, q in spots:
            tile = tile_at(step, q)
            sums.append(
                pick_product(
                    source,
                    [columns[k, tile] for k in range(depth)],
                    [panels[step * 4 + q, k] for k in range(depth)],
                )
            )
        for i, ((step, q), total) in enumerate(zip(spots, sums)):
            tile = tile_at(step, q)
            lanes = pl.ds(pl.multiple_of(tile * width, width), width)
            own = rhs[:, :, lanes].reshape(total.shape)
            done = solve_block(own, total, inverse[tile])
            solved[slot, i // 4, :, :, q * width : (q + 1) * width] = done.reshape(
                groups, rows, width
            )
        out_copy(turn).start()

    for i in range(2):
        pltpu.make_async_copy(
            solved.at[i], out.at[pl.ds(i * TOGETHER, TOGETHER)], out_sems.at[i]
        ).wait()


def leaf_part(
    part, found, level, rhs, panels, inverse, order, columns
):
    keys = tuple(sorted(key for key in found if key[1] in part))
    pieces = [found[key] for key in keys]
    blocks, rows, width = pieces[0].shape
    groups = 4 * len(part)
    tiles, depth = panels.shape[:2]
    level_blocks = 16
    return pl.pallas_call(
        functools.partial(leaf_kernel, part, keys),
        out_shape=jax.ShapeDtypeStruct(
            (level_blocks, groups, rows, 4 * width), jnp.bfloat16
        ),
        in_specs=[SMEM] * 2 + [ANY] * (len(keys) + 19),
        out_specs=ANY,
        scratch_shapes=[
            pltpu.VMEM((groups, 2 * blocks + level_blocks, rows, width), jnp.bfloat16),
            pltpu.VMEM((groups, rows, tiles * width), jnp.bfloat16),
            pltpu.VMEM((tiles, width, width), jnp.bfloat16),
            pltpu.VMEM((tiles, depth, width, width), jnp.bfloat16),
            pltpu.VMEM((2, TOGETHER, groups, rows, 4 * width), jnp.bfloat16),
            pltpu.SemaphoreType.DMA((len(keys) + len(part) * (level_blocks + 1) + 1,)),
            pltpu.SemaphoreType.DMA((tiles,)),
            pltpu.SemaphoreType.DMA((2,)),
        ],
        compiler_params=pltpu.CompilerParams(vmem_limit_bytes=VMEM_LIMIT),
        cost_estimate=SMALL,
        name="leaf_part",
    )(
        order,
        columns,
        *pieces,
        *level,
        rhs.reshape(4, 4, rows, tiles * width),
        inverse,
        panels,
    )


def place_kernel(part, arrived, *refs):
    out, held, in_sems, out_sems = refs[-4:]
    count, groups, _, span = arrived.shape
    inward = [
        pltpu.make_async_copy(arrived.at[k], held.at[k], in_sems.at[k])
        for k in range(count)
    ]
    for copy in inward:
        copy.start()
    outward = []
    for k in range(count):
        inward[k].wait()
        for i, dz in enumerate(part):
            copy = pltpu.make_async_copy(
                held.at[k, pl.ds(4 * i, 4)],
                out.at[(k // 4) ^ dz, :, :, pl.ds(k * span, span)],
                out_sems.at[len(part) * k + i],
            )
            copy.start()
            outward.append(copy)
    for copy in outward:
        copy.wait()


def place_part(part, arrived, before):
    count, groups, rows, span = arrived.shape
    extra = [] if before is None else [before]
    return pl.pallas_call(
        functools.partial(place_kernel, part),
        out_shape=jax.ShapeDtypeStruct((4, 4, rows, count * span), jnp.bfloat16),
        in_specs=[ANY] * (1 + len(extra)),
        out_specs=ANY,
        scratch_shapes=[
            pltpu.VMEM((count, groups, rows, span), jnp.bfloat16),
            pltpu.SemaphoreType.DMA((count,)),
            pltpu.SemaphoreType.DMA((count * len(part),)),
        ],
        input_output_aliases={} if before is None else {1: 0},
        compiler_params=pltpu.CompilerParams(vmem_limit_bytes=VMEM_LIMIT),
        cost_estimate=SMALL,
        name="place_part",
    )(arrived, *extra)


def on_device_pairs(
    root_rhs,
    root_inverse,
    level_rhs,
    level_inverse,
    level_panels,
    level_columns,
    leaf_rhs,
    leaf_inverse,
    leaf_panels,
    leaf_columns,
    slab_order,
):
    width = leaf_panels.shape[2]
    piece = jnp.einsum(
        "rnj,nij->nri",
        root_rhs.reshape(root_rhs.shape[0], root_inverse.shape[0], width),
        root_inverse,
        preferred_element_type=jnp.float32,
    ).astype(jnp.bfloat16)
    leaf_columns = leaf_columns.T
    found = gather_root(piece)
    block = level_block(found, level_rhs, level_panels, level_inverse, level_columns)
    level = gather_level(block)

    def leaf_of(part):
        return leaf_part(
            part,
            found,
            level,
            leaf_rhs,
            leaf_panels,
            leaf_inverse,
            slab_order,
            leaf_columns,
        )

    def exchange(value):
        return lax.all_to_all(value, "dev", split_axis=0, concat_axis=0, tiled=True)

    out = None
    for part in PARTS:
        out = place_part(part, exchange(leaf_of(part)), out)
    return out.reshape(leaf_rhs.shape)


def load_source(copies):
    for copy in copies:
        copy.start()
    for copy in copies:
        copy.wait()


def level_kernel_any(columns, root_hbm, rhs, panels, inverse, out, source, sems):
    subs, groups, blocks = root_hbm.shape[:3]
    copies = []
    for s in range(subs):
        for e in range(groups):
            copies.append(
                pltpu.make_async_copy(
                    root_hbm.at[s, e],
                    source.at[e, pl.ds(s * blocks, blocks)],
                    sems.at[s * groups + e],
                )
            )
    load_source(copies)
    tiles = panels.shape[1]
    part = pick_product(
        source,
        [columns[0, k] for k in range(tiles)],
        [panels[0, k] for k in range(tiles)],
    )
    shape = rhs.shape
    solved = solve_block(rhs[...].reshape(part.shape), part, inverse[0])
    out[...] = solved.reshape(shape)


def level_solve(root, rhs, panels, inverse, columns):
    subs, groups, blocks, rows, width = root.shape
    vmem = pl.BlockSpec(memory_space=pltpu.VMEM)
    return pl.pallas_call(
        level_kernel_any,
        out_shape=jax.ShapeDtypeStruct((groups, rows, width), jnp.bfloat16),
        in_specs=[
            pl.BlockSpec(memory_space=pltpu.SMEM),
            pl.BlockSpec(memory_space=pl.ANY),
            vmem,
            vmem,
            vmem,
        ],
        out_specs=vmem,
        scratch_shapes=[
            pltpu.VMEM((groups, subs * blocks, rows, width), jnp.bfloat16),
            pltpu.SemaphoreType.DMA((subs * groups,)),
        ],
        compiler_params=pltpu.CompilerParams(vmem_limit_bytes=40 * 2**20),
        name="level_solve",
    )(columns, root, rhs.reshape(groups, rows, width), panels, inverse)


def leaf_kernel_any(per_step, order, columns, root_hbm, level_hbm, *refs):
    rhs = refs[:per_step]
    panels = refs[per_step : 2 * per_step]
    inverse = refs[2 * per_step : 3 * per_step]
    out, source, sems = refs[3 * per_step :]
    subs, groups, blocks = root_hbm.shape[:3]
    level_blocks = level_hbm.shape[0]
    step = pl.program_id(0)

    @pl.when(step == 0)
    def _():
        copies = []
        for s in range(subs):
            for e in range(groups):
                copies.append(
                    pltpu.make_async_copy(
                        root_hbm.at[s, e],
                        source.at[e, pl.ds(s * blocks, blocks)],
                        sems.at[s * groups + e],
                    )
                )
        for j in range(level_blocks):
            copies.append(
                pltpu.make_async_copy(
                    level_hbm.at[j],
                    source.at[:, subs * blocks + j],
                    sems.at[subs * groups + j],
                )
            )
        load_source(copies)

    depth = panels[0].shape[1]
    groups, _, rows, width = source.shape
    for q in range(per_step):
        tile = order[0, step * per_step + q]
        part = pick_product(
            source,
            [columns[tile, k] for k in range(depth)],
            [panels[q][0, k] for k in range(depth)],
        )
        solved = solve_block(rhs[q][...].reshape(part.shape), part, inverse[q][0])
        out[0, :, :, q * width : (q + 1) * width] = solved.reshape(groups, rows, width)


def leaf_solve(root, level, rhs, panels, inverse, order, columns, peers):
    subs, groups, blocks, rows, width = root.shape
    tiles, depth = panels.shape[:2]
    per_step = tiles // peers
    level_blocks = level.shape[0]
    rhs = rhs.reshape(groups, rows, tiles * width)

    def tile_of(q):
        return lambda i, order, columns: order[0, i * per_step + q]

    def spec(shape, index):
        return [
            pl.BlockSpec(shape, functools.partial(index, q)) for q in range(per_step)
        ]

    def rhs_index(q, i, order, columns):
        return (0, 0, order[0, i * per_step + q])

    def panel_index(q, i, order, columns):
        return (order[0, i * per_step + q], 0, 0, 0)

    def inverse_index(q, i, order, columns):
        return (order[0, i * per_step + q], 0, 0)

    return pl.pallas_call(
        functools.partial(leaf_kernel_any, per_step),
        out_shape=jax.ShapeDtypeStruct(
            (peers, groups, rows, per_step * width), jnp.bfloat16
        ),
        grid_spec=pltpu.PrefetchScalarGridSpec(
            num_scalar_prefetch=2,
            grid=(peers,),
            in_specs=[pl.BlockSpec(memory_space=pl.ANY)] * 2
            + spec((groups, rows, width), rhs_index)
            + spec((1, depth, width, width), panel_index)
            + spec((1, width, width), inverse_index),
            out_specs=pl.BlockSpec(
                (1, groups, rows, per_step * width),
                lambda i, order, columns: (i, 0, 0, 0),
            ),
            scratch_shapes=[
                pltpu.VMEM(
                    (groups, subs * blocks + level_blocks, rows, width), jnp.bfloat16
                ),
                pltpu.SemaphoreType.DMA((subs * groups + level_blocks,)),
            ],
        ),
        compiler_params=pltpu.CompilerParams(vmem_limit_bytes=48 * 2**20),
        name="leaf_solve",
    )(
        order,
        columns,
        root,
        level,
        *([rhs] * per_step),
        *([panels] * per_step),
        *([inverse] * per_step),
    )


def on_device_any(
    root_rhs,
    root_inverse,
    level_rhs,
    level_inverse,
    level_panels,
    level_columns,
    leaf_rhs,
    leaf_inverse,
    leaf_panels,
    leaf_columns,
    slab_order,
):
    width = leaf_panels.shape[2]
    subs, peers = lax.axis_size("sub"), lax.axis_size("dev")
    row_count = leaf_rhs.shape[0]
    piece_rows = root_rhs.shape[0]
    blocks = root_inverse.shape[0]
    piece = jnp.einsum(
        "rnj,nij->nri",
        root_rhs.reshape(piece_rows, blocks, width),
        root_inverse,
        preferred_element_type=jnp.float32,
    ).astype(jnp.bfloat16)
    root = lax.all_gather(piece, ("sub", "dev"), axis=0, tiled=False)
    root = root.reshape(subs, peers, blocks, piece_rows, width)
    if piece_rows % 16:
        root = root.transpose(0, 2, 1, 3, 4).reshape(subs, 1, blocks, row_count, width)
    level = level_solve(root, level_rhs, level_panels, level_inverse, level_columns)
    level = lax.all_gather(level, "dev", axis=0, tiled=False)
    outgoing = leaf_solve(
        root, level, leaf_rhs, leaf_panels, leaf_inverse, slab_order, leaf_columns, peers
    )
    outgoing = outgoing.reshape(peers, row_count, -1)
    arrived = lax.all_to_all(outgoing, "dev", split_axis=0, concat_axis=0, tiled=True)
    return arrived.transpose(1, 0, 2).reshape(row_count, -1)


def solution(mesh):
    in_specs = (
        P("dev", "sub"),
        P("sub", None, None),
        P(None, ("sub", "dev")),
        P(("sub", "dev"), None, None),
        P(("sub", "dev"), None, None, None),
        P(("sub", "dev"), None),
        P(None, ("sub", "dev")),
        P(("sub", "dev"), None, None),
        P(("sub", "dev"), None, None, None),
        P(("sub", "dev"), None),
        P(("sub", "dev"), None),
    )
    out_specs = P(None, ("sub", "dev"))
    fits = mesh.shape["sub"] == 2 and mesh.shape["dev"] == 16
    on_device = on_device_pairs if fits else on_device_any
    return jax.shard_map(
        on_device, mesh=mesh, in_specs=in_specs, out_specs=out_specs, check_vma=False
    )
```

```python
import functools

import jax
import jax.numpy as jnp
from jax import lax
from jax.experimental import pallas as pl
from jax.experimental.pallas import tpu as pltpu
from jax.sharding import PartitionSpec as P

NT = (((1,), (1,)), ((), ()))
ANY = pl.BlockSpec(memory_space=pltpu.HBM)
SMEM = pl.BlockSpec(memory_space=pltpu.SMEM)
VMEM_LIMIT = 60 * 2**20
TOGETHER = 2
PARTS = ((0, 1), (2, 3))
SMALL = pl.CostEstimate(flops=1000, bytes_accessed=1000, transcendentals=0)


def pick_product(source, columns, panels):
    groups, _, rows, width = source.shape
    picked = [source[:, col].reshape(groups * rows, width) for col in columns]
    total = None
    step = 2 if len(picked) % 2 == 0 else 1
    for k in range(0, len(picked), step):
        left = jnp.concatenate(picked[k : k + step], axis=1)
        right = jnp.concatenate(panels[k : k + step], axis=1)
        term = lax.dot_general(left, right, NT, preferred_element_type=jnp.float32)
        total = term if total is None else total + term
    return total


def solve_block(rhs, part, inverse):
    residue = (rhs.astype(jnp.float32) - part).astype(jnp.bfloat16)
    return lax.dot_general(
        residue, inverse, NT, preferred_element_type=jnp.float32
    ).astype(jnp.bfloat16)


def run_copies(pairs, sems):
    copies = [
        pltpu.make_async_copy(src, dst, sems.at[i]) for i, (src, dst) in enumerate(pairs)
    ]
    for copy in copies:
        copy.start()
    for copy in copies:
        copy.wait()


def flat_permute(value, dx=0, dz=0, dy=0, dc=0):
    step = dx * 16 + dz * 4 + dy * 2 + dc
    return lax.ppermute(value, ("sub", "dev"), [(i, i ^ step) for i in range(32)])


def after(values, event):
    return lax.optimization_barrier((values, event))[0]


SIDES = ((0, 0), (1, 0), (0, 1), (1, 1))


def gather_root(piece):
    found = {}

    def plane(dz, base, x_first):
        from_x = flat_permute(base, dx=1)
        from_y = flat_permute(base, dy=1)
        if x_first:
            corner = flat_permute(from_x, dy=1)
        else:
            corner = flat_permute(from_y, dx=1)
        for (dx, dy), value in zip(SIDES, (base, from_x, from_y, corner)):
            found[dx, dz, dy, 0] = value
        return from_x, from_y

    near = flat_permute(piece, dz=1)
    far = flat_permute(piece, dz=2)
    sides = plane(0, piece, True)
    last = flat_permute(after(piece, sides), dz=3)
    sides = plane(1, after(near, sides), False)
    sides = plane(2, after(far, sides), True)
    plane(3, after(last, sides), False)
    for key in tuple(found):
        found[key[:3] + (1,)] = flat_permute(found[key], dc=1)
    return found


def piece_pairs(keys, pieces, source, groups):
    me_sub, me_dev = lax.axis_index("sub"), lax.axis_index("dev")
    pairs = []
    for (dx, dz, dy, dc), piece in zip(keys, pieces):
        blocks = piece.shape[0]
        group = (me_dev ^ (dz * 4 + dy * 2 + dc)) % groups
        pairs.append((piece, source.at[group, pl.ds((me_sub ^ dx) * blocks, blocks)]))
    return pairs


def level_kernel(keys, columns, *refs):
    count = len(keys)
    pieces = refs[:count]
    rhs, panels, inverse, out, source, sems = refs[count:]
    run_copies(piece_pairs(keys, pieces, source, source.shape[0]), sems)
    tiles = panels.shape[1]
    part = pick_product(
        source,
        [columns[0, k] for k in range(tiles)],
        [panels[0, k] for k in range(tiles)],
    )
    solved = solve_block(rhs[...], part, inverse[0])
    out[...] = solved.reshape(out.shape)


def level_block(found, rhs, panels, inverse, columns):
    keys = tuple(sorted(found, key=lambda key: key[1]))
    pieces = [found[key] for key in keys]
    blocks, rows, width = pieces[0].shape
    vmem = pl.BlockSpec(memory_space=pltpu.VMEM)
    return pl.pallas_call(
        functools.partial(level_kernel, keys),
        out_shape=jax.ShapeDtypeStruct((16, rows, width), jnp.bfloat16),
        in_specs=[SMEM] + [ANY] * len(keys) + [vmem] * 3,
        out_specs=vmem,
        scratch_shapes=[
            pltpu.VMEM((16, 2 * blocks, rows, width), jnp.bfloat16),
            pltpu.SemaphoreType.DMA((len(keys),)),
        ],
        compiler_params=pltpu.CompilerParams(vmem_limit_bytes=VMEM_LIMIT),
        cost_estimate=SMALL,
        name="level_block",
    )(columns, *pieces, rhs, panels, inverse)


def swap_cores(value):
    return lax.ppermute(value, "dev", [(i, i ^ 1) for i in range(16)])


def gather_level(block):
    mine = [block]
    for k in range(2, 16, 2):
        mine.append(lax.ppermute(block, "dev", [(i, i ^ k) for i in range(16)]))
    return mine + [swap_cores(value) for value in mine]


def leaf_kernel(part, keys, order, columns, *refs):
    count = len(keys)
    pieces = refs[:count]
    level = refs[count : count + 16]
    rhs_hbm, inverse_hbm, panels_hbm = refs[count + 16 : count + 19]
    out, source, rhs, inverse, panels, solved, sems, tile_sems, out_sems = refs[
        count + 19 :
    ]
    steps = out.shape[0]
    me_dev = lax.axis_index("dev")
    chip, core = me_dev // 2, me_dev % 2
    first = source.shape[1] - steps

    def tile_at(step, q):
        return order[0, step * 4 + q]

    groups, _, rows, width = source.shape
    z = me_dev // 4
    pairs = []
    for (dx, dz, dy, dc), piece in zip(keys, pieces):
        group = 4 * part.index(dz) + (me_dev ^ (2 * dy + dc)) % 4
        blocks = piece.shape[0]
        begin = (lax.axis_index("sub") ^ dx) * blocks
        pairs.append((piece, source.at[group, pl.ds(begin, blocks)]))
    for place, dz in enumerate(part):
        spot, mine = pl.ds(4 * place, 4), pl.ds((z ^ dz) * 4, 4)
        for i in range(8):
            owner = first + (chip ^ i) * 2
            pairs.append((level[i].at[mine], source.at[spot, owner + core]))
            pairs.append((level[8 + i].at[mine], source.at[spot, owner + 1 - core]))

    def panel_copy(step, q):
        spot = step * 4 + q
        return pltpu.make_async_copy(
            panels_hbm.at[tile_at(step, q)], panels.at[spot], tile_sems.at[spot]
        )

    copies = [
        pltpu.make_async_copy(src, dst, sems.at[i]) for i, (src, dst) in enumerate(pairs)
    ]
    for copy in copies:
        copy.start()

    for step in range(TOGETHER):
        for q in range(4):
            panel_copy(step, q).start()
    shared = [
        pltpu.make_async_copy(inverse_hbm, inverse, sems.at[len(pairs)]),
    ]
    shared += [
        pltpu.make_async_copy(
            rhs_hbm.at[z ^ dz], rhs.at[pl.ds(4 * i, 4)], sems.at[len(pairs) + 1 + i]
        )
        for i, dz in enumerate(part)
    ]
    for copy in shared:
        copy.start()

    @pl.loop(TOGETHER, steps)
    def _(step):
        for q in range(4):
            panel_copy(step, q).start()

    for copy in copies + shared:
        copy.wait()

    depth = panels.shape[1]

    @pl.loop(0, steps // TOGETHER)
    def _(turn):
        slot = lax.rem(turn, 2)
        spots = [(turn * TOGETHER + i, q) for i in range(TOGETHER) for q in range(4)]

        def out_copy(turn):
            return pltpu.make_async_copy(
                solved.at[slot],
                out.at[pl.ds(turn * TOGETHER, TOGETHER)],
                out_sems.at[slot],
            )

        @pl.when(turn >= 2)
        def _():
            out_copy(turn).wait()

        for step, q in spots:
            panel_copy(step, q).wait()
        sums = []
        for step, q in spots:
            tile = tile_at(step, q)
            sums.append(
                pick_product(
                    source,
                    [columns[k, tile] for k in range(depth)],
                    [panels[step * 4 + q, k] for k in range(depth)],
                )
            )
        for i, ((step, q), total) in enumerate(zip(spots, sums)):
            tile = tile_at(step, q)
            lanes = pl.ds(pl.multiple_of(tile * width, width), width)
            own = rhs[:, :, lanes].reshape(total.shape)
            done = solve_block(own, total, inverse[tile])
            solved[slot, i // 4, :, :, q * width : (q + 1) * width] = done.reshape(
                groups, rows, width
            )
        out_copy(turn).start()

    for i in range(2):
        pltpu.make_async_copy(
            solved.at[i], out.at[pl.ds(i * TOGETHER, TOGETHER)], out_sems.at[i]
        ).wait()


def leaf_part(
    part, found, level, rhs, panels, inverse, order, columns
):
    keys = tuple(sorted(key for key in found if key[1] in part))
    pieces = [found[key] for key in keys]
    blocks, rows, width = pieces[0].shape
    groups = 4 * len(part)
    tiles, depth = panels.shape[:2]
    level_blocks = 16
    return pl.pallas_call(
        functools.partial(leaf_kernel, part, keys),
        out_shape=jax.ShapeDtypeStruct(
            (level_blocks, groups, rows, 4 * width), jnp.bfloat16
        ),
        in_specs=[SMEM] * 2 + [ANY] * (len(keys) + 19),
        out_specs=ANY,
        scratch_shapes=[
            pltpu.VMEM((groups, 2 * blocks + level_blocks, rows, width), jnp.bfloat16),
            pltpu.VMEM((groups, rows, tiles * width), jnp.bfloat16),
            pltpu.VMEM((tiles, width, width), jnp.bfloat16),
            pltpu.VMEM((tiles, depth, width, width), jnp.bfloat16),
            pltpu.VMEM((2, TOGETHER, groups, rows, 4 * width), jnp.bfloat16),
            pltpu.SemaphoreType.DMA((len(keys) + len(part) * (level_blocks + 1) + 1,)),
            pltpu.SemaphoreType.DMA((tiles,)),
            pltpu.SemaphoreType.DMA((2,)),
        ],
        compiler_params=pltpu.CompilerParams(vmem_limit_bytes=VMEM_LIMIT),
        cost_estimate=SMALL,
        name="leaf_part",
    )(
        order,
        columns,
        *pieces,
        *level,
        rhs.reshape(4, 4, rows, tiles * width),
        inverse,
        panels,
    )


def place_kernel(part, arrived, *refs):
    out, held, in_sems, out_sems = refs[-4:]
    count, groups, _, span = arrived.shape
    inward = [
        pltpu.make_async_copy(arrived.at[k], held.at[k], in_sems.at[k])
        for k in range(count)
    ]
    for copy in inward:
        copy.start()
    outward = []
    for k in range(count):
        inward[k].wait()
        for i, dz in enumerate(part):
            copy = pltpu.make_async_copy(
                held.at[k, pl.ds(4 * i, 4)],
                out.at[(k // 4) ^ dz, :, :, pl.ds(k * span, span)],
                out_sems.at[len(part) * k + i],
            )
            copy.start()
            outward.append(copy)
    for copy in outward:
        copy.wait()


def place_part(part, arrived, before):
    count, groups, rows, span = arrived.shape
    extra = [] if before is None else [before]
    return pl.pallas_call(
        functools.partial(place_kernel, part),
        out_shape=jax.ShapeDtypeStruct((4, 4, rows, count * span), jnp.bfloat16),
        in_specs=[ANY] * (1 + len(extra)),
        out_specs=ANY,
        scratch_shapes=[
            pltpu.VMEM((count, groups, rows, span), jnp.bfloat16),
            pltpu.SemaphoreType.DMA((count,)),
            pltpu.SemaphoreType.DMA((count * len(part),)),
        ],
        input_output_aliases={} if before is None else {1: 0},
        compiler_params=pltpu.CompilerParams(vmem_limit_bytes=VMEM_LIMIT),
        cost_estimate=SMALL,
        name="place_part",
    )(arrived, *extra)


def place_each_kernel(part, *refs):
    count = 16
    arrived = refs[:count]
    out, held, in_sems, out_sems = refs[-4:]
    span = held.shape[4]
    me_dev = lax.axis_index("dev")
    inward = [
        pltpu.make_async_copy(arrived[k], held.at[k], in_sems.at[k])
        for k in range(count)
    ]
    for copy in inward:
        copy.start()
    outward = []
    for k in range(count):
        inward[k].wait()
        owner = me_dev ^ k
        columns = pl.ds(pl.multiple_of(owner * span, span), span)
        for i, dz in enumerate(part):
            copy = pltpu.make_async_copy(
                held.at[k, 0, pl.ds(4 * i, 4)],
                out.at[(owner // 4) ^ dz, :, :, columns],
                out_sems.at[len(part) * k + i],
            )
            copy.start()
            outward.append(copy)
    for copy in outward:
        copy.wait()


def place_each(part, arrived, before):
    count = len(arrived)
    return pl.pallas_call(
        functools.partial(place_each_kernel, part),
        out_shape=jax.ShapeDtypeStruct(before.shape, jnp.bfloat16),
        in_specs=[ANY] * (count + 1),
        out_specs=ANY,
        scratch_shapes=[
            pltpu.VMEM((count,) + arrived[0].shape, jnp.bfloat16),
            pltpu.SemaphoreType.DMA((count,)),
            pltpu.SemaphoreType.DMA((count * len(part),)),
        ],
        input_output_aliases={count: 0},
        compiler_params=pltpu.CompilerParams(vmem_limit_bytes=VMEM_LIMIT),
        cost_estimate=SMALL,
        name="place_each",
    )(*arrived, before)


SEND_ORDER = (12, 3, 13, 4, 14, 2, 15, 5, 8, 1, 9, 6, 10, 7, 11)


def on_device_pairs(
    root_rhs,
    root_inverse,
    level_rhs,
    level_inverse,
    level_panels,
    level_columns,
    leaf_rhs,
    leaf_inverse,
    leaf_panels,
    leaf_columns,
    slab_order,
):
    width = leaf_panels.shape[2]
    piece = jnp.einsum(
        "rnj,nij->nri",
        root_rhs.reshape(root_rhs.shape[0], root_inverse.shape[0], width),
        root_inverse,
        preferred_element_type=jnp.float32,
    ).astype(jnp.bfloat16)
    leaf_columns = leaf_columns.T
    found = gather_root(piece)
    block = level_block(found, level_rhs, level_panels, level_inverse, level_columns)
    level = gather_level(block)

    def leaf_of(part):
        return leaf_part(
            part,
            found,
            level,
            leaf_rhs,
            leaf_panels,
            leaf_inverse,
            slab_order,
            leaf_columns,
        )

    def exchange(value):
        return lax.all_to_all(value, "dev", split_axis=0, concat_axis=0, tiled=True)

    out = place_part(PARTS[0], exchange(leaf_of(PARTS[0])), None)
    solved = leaf_of(PARTS[1])
    me_dev = lax.axis_index("dev")
    arrived = [lax.dynamic_slice_in_dim(solved, me_dev, 1)] + [None] * 15
    for k in SEND_ORDER:
        value = lax.dynamic_slice_in_dim(solved, me_dev ^ k, 1)
        arrived[k] = lax.ppermute(value, "dev", [(i, i ^ k) for i in range(16)])
    out = place_each(PARTS[1], arrived, out)
    return out.reshape(leaf_rhs.shape)


def load_source(copies):
    for copy in copies:
        copy.start()
    for copy in copies:
        copy.wait()


def level_kernel_any(columns, root_hbm, rhs, panels, inverse, out, source, sems):
    subs, groups, blocks = root_hbm.shape[:3]
    copies = []
    for s in range(subs):
        for e in range(groups):
            copies.append(
                pltpu.make_async_copy(
                    root_hbm.at[s, e],
                    source.at[e, pl.ds(s * blocks, blocks)],
                    sems.at[s * groups + e],
                )
            )
    load_source(copies)
    tiles = panels.shape[1]
    part = pick_product(
        source,
        [columns[0, k] for k in range(tiles)],
        [panels[0, k] for k in range(tiles)],
    )
    shape = rhs.shape
    solved = solve_block(rhs[...].reshape(part.shape), part, inverse[0])
    out[...] = solved.reshape(shape)


def level_solve(root, rhs, panels, inverse, columns):
    subs, groups, blocks, rows, width = root.shape
    vmem = pl.BlockSpec(memory_space=pltpu.VMEM)
    return pl.pallas_call(
        level_kernel_any,
        out_shape=jax.ShapeDtypeStruct((groups, rows, width), jnp.bfloat16),
        in_specs=[
            pl.BlockSpec(memory_space=pltpu.SMEM),
            pl.BlockSpec(memory_space=pl.ANY),
            vmem,
            vmem,
            vmem,
        ],
        out_specs=vmem,
        scratch_shapes=[
            pltpu.VMEM((groups, subs * blocks, rows, width), jnp.bfloat16),
            pltpu.SemaphoreType.DMA((subs * groups,)),
        ],
        compiler_params=pltpu.CompilerParams(vmem_limit_bytes=40 * 2**20),
        name="level_solve",
    )(columns, root, rhs.reshape(groups, rows, width), panels, inverse)


def leaf_kernel_any(per_step, order, columns, root_hbm, level_hbm, *refs):
    rhs = refs[:per_step]
    panels = refs[per_step : 2 * per_step]
    inverse = refs[2 * per_step : 3 * per_step]
    out, source, sems = refs[3 * per_step :]
    subs, groups, blocks = root_hbm.shape[:3]
    level_blocks = level_hbm.shape[0]
    step = pl.program_id(0)

    @pl.when(step == 0)
    def _():
        copies = []
        for s in range(subs):
            for e in range(groups):
                copies.append(
                    pltpu.make_async_copy(
                        root_hbm.at[s, e],
                        source.at[e, pl.ds(s * blocks, blocks)],
                        sems.at[s * groups + e],
                    )
                )
        for j in range(level_blocks):
            copies.append(
                pltpu.make_async_copy(
                    level_hbm.at[j],
                    source.at[:, subs * blocks + j],
                    sems.at[subs * groups + j],
                )
            )
        load_source(copies)

    depth = panels[0].shape[1]
    groups, _, rows, width = source.shape
    for q in range(per_step):
        tile = order[0, step * per_step + q]
        part = pick_product(
            source,
            [columns[tile, k] for k in range(depth)],
            [panels[q][0, k] for k in range(depth)],
        )
        solved = solve_block(rhs[q][...].reshape(part.shape), part, inverse[q][0])
        out[0, :, :, q * width : (q + 1) * width] = solved.reshape(groups, rows, width)


def leaf_solve(root, level, rhs, panels, inverse, order, columns, peers):
    subs, groups, blocks, rows, width = root.shape
    tiles, depth = panels.shape[:2]
    per_step = tiles // peers
    level_blocks = level.shape[0]
    rhs = rhs.reshape(groups, rows, tiles * width)

    def tile_of(q):
        return lambda i, order, columns: order[0, i * per_step + q]

    def spec(shape, index):
        return [
            pl.BlockSpec(shape, functools.partial(index, q)) for q in range(per_step)
        ]

    def rhs_index(q, i, order, columns):
        return (0, 0, order[0, i * per_step + q])

    def panel_index(q, i, order, columns):
        return (order[0, i * per_step + q], 0, 0, 0)

    def inverse_index(q, i, order, columns):
        return (order[0, i * per_step + q], 0, 0)

    return pl.pallas_call(
        functools.partial(leaf_kernel_any, per_step),
        out_shape=jax.ShapeDtypeStruct(
            (peers, groups, rows, per_step * width), jnp.bfloat16
        ),
        grid_spec=pltpu.PrefetchScalarGridSpec(
            num_scalar_prefetch=2,
            grid=(peers,),
            in_specs=[pl.BlockSpec(memory_space=pl.ANY)] * 2
            + spec((groups, rows, width), rhs_index)
            + spec((1, depth, width, width), panel_index)
            + spec((1, width, width), inverse_index),
            out_specs=pl.BlockSpec(
                (1, groups, rows, per_step * width),
                lambda i, order, columns: (i, 0, 0, 0),
            ),
            scratch_shapes=[
                pltpu.VMEM(
                    (groups, subs * blocks + level_blocks, rows, width), jnp.bfloat16
                ),
                pltpu.SemaphoreType.DMA((subs * groups + level_blocks,)),
            ],
        ),
        compiler_params=pltpu.CompilerParams(vmem_limit_bytes=48 * 2**20),
        name="leaf_solve",
    )(
        order,
        columns,
        root,
        level,
        *([rhs] * per_step),
        *([panels] * per_step),
        *([inverse] * per_step),
    )


def on_device_any(
    root_rhs,
    root_inverse,
    level_rhs,
    level_inverse,
    level_panels,
    level_columns,
    leaf_rhs,
    leaf_inverse,
    leaf_panels,
    leaf_columns,
    slab_order,
):
    width = leaf_panels.shape[2]
    subs, peers = lax.axis_size("sub"), lax.axis_size("dev")
    row_count = leaf_rhs.shape[0]
    piece_rows = root_rhs.shape[0]
    blocks = root_inverse.shape[0]
    piece = jnp.einsum(
        "rnj,nij->nri",
        root_rhs.reshape(piece_rows, blocks, width),
        root_inverse,
        preferred_element_type=jnp.float32,
    ).astype(jnp.bfloat16)
    root = lax.all_gather(piece, ("sub", "dev"), axis=0, tiled=False)
    root = root.reshape(subs, peers, blocks, piece_rows, width)
    if piece_rows % 16:
        root = root.transpose(0, 2, 1, 3, 4).reshape(subs, 1, blocks, row_count, width)
    level = level_solve(root, level_rhs, level_panels, level_inverse, level_columns)
    level = lax.all_gather(level, "dev", axis=0, tiled=False)
    outgoing = leaf_solve(
        root, level, leaf_rhs, leaf_panels, leaf_inverse, slab_order, leaf_columns, peers
    )
    outgoing = outgoing.reshape(peers, row_count, -1)
    arrived = lax.all_to_all(outgoing, "dev", split_axis=0, concat_axis=0, tiled=True)
    return arrived.transpose(1, 0, 2).reshape(row_count, -1)


def solution(mesh):
    in_specs = (
        P("dev", "sub"),
        P("sub", None, None),
        P(None, ("sub", "dev")),
        P(("sub", "dev"), None, None),
        P(("sub", "dev"), None, None, None),
        P(("sub", "dev"), None),
        P(None, ("sub", "dev")),
        P(("sub", "dev"), None, None),
        P(("sub", "dev"), None, None, None),
        P(("sub", "dev"), None),
        P(("sub", "dev"), None),
    )
    out_specs = P(None, ("sub", "dev"))
    fits = mesh.shape["sub"] == 2 and mesh.shape["dev"] == 16
    on_device = on_device_pairs if fits else on_device_any
    return jax.shard_map(
        on_device, mesh=mesh, in_specs=in_specs, out_specs=out_specs, check_vma=False
    )
```
